128 devices in a mesh: role: 2 (over core), dev: 64 (over x, y, z).
Axes of the slice: x: 4, y: 4, z: 4, core: 2. Of those that a mesh axis runs over, the one named last changes fastest.
Arguments:
- tokens: bfloat16 [16384, 3584], P(('role', 'dev')), may hold values from -6 to 6
- grad_out: bfloat16 [16384, 3584], P(('role', 'dev')), may hold values from -6 to 6
- routes: int32 [16384, 4], P(('role', 'dev')), may hold values from 0 to 127, all different within a row; in each aligned block of 128 rows (0 to 127, 128 to 255, ...) at most 5 rows name the same one
- gates: float32 [16384, 4], P(('role', 'dev')), may hold values from 0.1 to 0.8
- gate_weight: bfloat16 [128, 3584, 1024], P(('role', 'dev')), may hold values from -0.09375 to 0.09375
- up_weight: bfloat16 [128, 3584, 1024], P(('role', 'dev')), may hold values from -0.09375 to 0.09375
- down_weight: bfloat16 [128, 1024, 3584], P(('role', 'dev')), may hold values from -0.1875 to 0.1875
Outputs:
- layer_out: bfloat16 [16384, 3584], P(('role', 'dev'))
- grad_in: bfloat16 [16384, 3584], P(('role', 'dev'))
The draws below stay inside these ranges and needn't reach their ends.
Inputs may be any that keep to these rules, and one draw needn't show every extreme that they name: `routes`: within the 4 entries of a token the experts differ. In the rows of one device (aligned blocks of 128 tokens) no expert is named more than 5 times, a bound that some block reaches.
All inputs are finite; a program needn't handle non-finite values.
Results may differ from the reference program's by a relative error of at most 0.006.
Values may be sent and summed in bfloat16 or wider, within the bound.
No kernel may reach another device: no remote copies, remote signals or barrier semaphores. Data moves between devices by JAX's collectives and lax.ppermute only.
A program may use at most 128 MiB of HBM per device.

```python
import math
import jax
import jax.numpy as jnp
import numpy as np
from jax import lax

D = 3584
FFE = 1024
TOP = 4
TOK_DEV = 128
EXPERTS = 128
TOKENS = 16384
CAP = 5


def block_levels(key, shape, cuts, low, high):
    def one(position, shards_of):
        steps = jax.random.uniform(jax.random.fold_in(jax.random.fold_in(key, 6), position), (shards_of,), jnp.float32, low / len(cuts), high / len(cuts))
        return jnp.repeat(jnp.exp(steps), shape[position] // shards_of).reshape((-1,) + (1,) * (len(shape) - position - 1))

    gain = one(*cuts[0])
    for cut in cuts[1:]:
        gain = gain * one(*cut)
    return gain


def deal_out(key, own, number, rows, number_of, top, bound, lean):
    ranking = jax.random.permutation(key, number_of)
    heavy_load, common = shares(number_of, rows * top, bound, lean, True), shares(number_of, rows * top, bound, lean, False)
    places = jnp.arange(number_of)

    def named(tallies, offset_by):
        used = int((tallies > 0).sum())
        fixed = max(1, used // 4)
        shifted = fixed + (places - fixed + offset_by * (used - fixed)) % max(1, number_of - fixed)
        return jnp.zeros((number_of,), jnp.int32).at[ranking[jnp.where(places < fixed, places, shifted)]].set(jnp.asarray(tallies, jnp.int32))

    tallies = jnp.where(number % 4 == 0, named(heavy_load, number // 4), named(common, number - number // 4 - 1))
    mixed = jax.random.permutation(jax.random.fold_in(own, 3), number_of)
    giver, receiver = mixed[0:number_of // 2 * 2:2], mixed[1:number_of // 2 * 2:2]
    room = jnp.minimum(tallies[giver] - 1, bound - tallies[receiver]) // 2
    room = jnp.where((giver == ranking[0]) | (receiver == ranking[0]) | (tallies[receiver] == 0), 0, jnp.maximum(room, 0))
    shifted = jax.random.randint(jax.random.fold_in(own, 4), (number_of // 2,), 0, 1 << 20) % (room + 1)
    tallies = tallies.at[giver].add(-shifted).at[receiver].add(shifted)
    labels = jnp.searchsorted(jnp.cumsum(tallies), jnp.arange(rows * top), side="right").astype(jnp.int32)
    grid = labels.reshape(top, rows).T
    grid = grid[jax.random.permutation(jax.random.fold_in(own, 1), rows)]
    offset_by = jax.random.randint(jax.random.fold_in(own, 2), (rows, 1), 0, top)
    return jnp.take_along_axis(grid, (jnp.arange(top)[None, :] + offset_by) % top, axis=1)


def shares(count, total, most, slope, full):
    weights = [(1 << 20) // math.isqrt(grade ** slope) + 1 for grade in range(1, count + 1)]
    largest = most if full else min(most, max(-(-total // count), total * weights[0] // sum(weights)))
    least = 1 if total - largest >= count - 1 else 0
    counts, surplus = [largest] + [least] * (count - 1), total - largest - least * (count - 1)
    while surplus > 0:
        free = [i for i in range(1, count) if counts[i] < largest] or [i for i in range(1, count) if counts[i] < most]
        pool, budget = sum([weights[i] for i in free]), surplus
        for i in free:
            addition = min(most - counts[i], max(1, budget * weights[i] // pool), surplus)
            counts[i] = counts[i] + addition
            surplus = surplus - addition
    return np.array(counts)


def normal_values(own_key, extent, scale, limit, cuts=(), held_as=jnp.bfloat16):
    array = scale * jax.random.normal(own_key, extent, jnp.float32)
    if cuts:
        array = array * block_levels(own_key, extent, cuts, -0.22, 0.18)
    return jnp.clip(array, -limit, limit).astype(held_as)


def setup_inputs(seed: int = 0) -> dict:
    arg_keys = jax.random.split(jax.random.key(seed), 8)
    tokens = normal_values(arg_keys[0], (TOKENS, D), 1.0, 6.0, ((0, 128),))
    grad_out = normal_values(arg_keys[1], (TOKENS, D), 1.0, 6.0, ((0, 128),))
    routes_keys = jax.random.split(jax.random.fold_in(arg_keys[2], 1), TOKENS // TOK_DEV)
    routes_turns = jax.random.permutation(jax.random.fold_in(arg_keys[2], 3), TOKENS // TOK_DEV)
    routes = jax.vmap(lambda own, number: deal_out(jax.random.fold_in(arg_keys[2], 2), own, number, TOK_DEV, EXPERTS, TOP, CAP, 2))(routes_keys, routes_turns).reshape((TOKENS, TOP))
    gates = jnp.clip(jnp.exp(math.log(0.8) - 2.0794415 * jax.random.uniform(arg_keys[3], (TOKENS, TOP), jnp.float32) ** block_levels(arg_keys[3], (TOKENS, TOP), ((0, 128),), -0.2, 0.2)), 0.1, 0.8)
    gate_weight = normal_values(arg_keys[4], (EXPERTS, D, FFE), D ** -0.5, 0.09375, ((0, 128),))
    up_weight = normal_values(arg_keys[5], (EXPERTS, D, FFE), D ** -0.5, 0.09375, ((0, 128),))
    down_weight = normal_values(arg_keys[6], (EXPERTS, FFE, D), FFE ** -0.5, 0.1875, ((0, 128),))
    return dict(tokens=tokens, grad_out=grad_out, routes=routes, gates=gates, gate_weight=gate_weight, up_weight=up_weight, down_weight=down_weight)


epsilon = 1e-06

def expert_rows(stacked, gate_weight, up_weight, down_weight):
    normed = stacked[:, 0]
    grad_scaled = stacked[:, 1]
    hidden_a = jnp.dot(normed, gate_weight, preferred_element_type=jnp.float32)
    hidden_b = jnp.dot(normed, up_weight, preferred_element_type=jnp.float32)
    sigmoid_a = jax.nn.sigmoid(hidden_a)
    silu_a = hidden_a * sigmoid_a
    product = (silu_a * hidden_b).astype(jnp.bfloat16)
    expert_out = jnp.dot(product, down_weight, preferred_element_type=jnp.float32).astype(jnp.bfloat16)
    contract = (((1,), (1,)), ((), ()))
    grad_act = lax.dot_general(grad_scaled, down_weight, contract, preferred_element_type=jnp.float32)
    silu_slope = sigmoid_a * (1.0 + hidden_a * (1.0 - sigmoid_a))
    grad_a = (grad_act * hidden_b * silu_slope).astype(jnp.bfloat16)
    grad_b = (grad_act * silu_a).astype(jnp.bfloat16)
    grad_rows = lax.dot_general(grad_a, gate_weight, contract, preferred_element_type=jnp.float32)
    grad_rows = grad_rows + lax.dot_general(grad_b, up_weight, contract, preferred_element_type=jnp.float32)
    return jnp.stack([expert_out, grad_rows.astype(jnp.bfloat16)], axis=1)

def reference(tokens, grad_out, routes, gates, gate_weight, up_weight, down_weight):
    features = tokens.shape[1]
    block_count = TOKENS // TOK_DEV
    flat_routes = routes.reshape(block_count, TOK_DEV * TOP).astype(jnp.int32)
    one_hot = (flat_routes[:, :, None] == jnp.arange(EXPERTS, dtype=jnp.int32)[None, None, :]).astype(jnp.int32)
    earlier = jnp.cumsum(one_hot, axis=1) - one_hot
    ranks = lax.optimization_barrier(jnp.sum(earlier * one_hot, axis=2)).astype(jnp.int32)
    owners = jnp.broadcast_to(jnp.arange(block_count, dtype=jnp.int32)[:, None], flat_routes.shape)
    entries = jnp.arange(TOKENS * TOP, dtype=jnp.int32).reshape(block_count, TOK_DEV * TOP)
    table = jnp.full((EXPERTS, block_count, CAP), TOKENS * TOP, dtype=jnp.int32)
    table = table.at[flat_routes, owners, ranks].set(entries).reshape(EXPERTS, block_count * CAP)
    tokens_wide = tokens.astype(jnp.float32)
    inv_rms = lax.rsqrt(lax.optimization_barrier(jnp.mean(tokens_wide * tokens_wide, axis=1, keepdims=True)) + epsilon)
    normed = (tokens_wide * inv_rms).astype(jnp.bfloat16)
    normed_ext = jnp.concatenate([normed, jnp.zeros((1, features), jnp.bfloat16)], axis=0)
    grad_ext = jnp.concatenate([grad_out.astype(jnp.float32), jnp.zeros((1, features), jnp.float32)], axis=0)
    gates_ext = jnp.concatenate([gates.reshape(-1).astype(jnp.float32), jnp.zeros((1,), jnp.float32)], axis=0)

    def expert_step(carry, inputs):
        slot_ids, gate_w, up_w, down_w = inputs
        token_ids = (slot_ids // TOP).astype(jnp.int32)
        gate_col = gates_ext[slot_ids][:, None]
        scaled = (gate_col * grad_ext[token_ids]).astype(jnp.bfloat16)
        stacked = jnp.stack([normed_ext[token_ids], scaled], axis=1)
        result = expert_rows(stacked, gate_w, up_w, down_w).astype(jnp.float32)
        out_sum, grad_sum = carry
        out_sum = out_sum.at[token_ids].add(gate_col * result[:, 0])
        grad_sum = grad_sum.at[token_ids].add(result[:, 1])
        return ((out_sum, grad_sum), None)
    start = (jnp.zeros((TOKENS + 1, features), jnp.float32), jnp.zeros((TOKENS + 1, features), jnp.float32))
    (out_sum, grad_sum), _ = lax.scan(expert_step, start, (table, gate_weight, up_weight, down_weight))
    layer_out = (tokens_wide + out_sum[:TOKENS]).astype(jnp.bfloat16)
    grad_normed = grad_sum[:TOKENS]
    projected = lax.optimization_barrier(jnp.mean(grad_normed * tokens_wide, axis=1, keepdims=True))
    grad_in = grad_out.astype(jnp.float32) + inv_rms * grad_normed - tokens_wide * inv_rms ** 3 * projected
    return (layer_out, grad_in.astype(jnp.bfloat16))
```

```python
import jax
import jax.numpy as jnp
import numpy as np
from jax import lax
from jax.experimental import pallas as pl
from jax.experimental.pallas import tpu as pltpu
from jax.sharding import PartitionSpec as P

epsilon = 1e-06
bf16, f32 = jnp.bfloat16, jnp.float32
CHUNKS = 4
BLOCK = 64
VMEM_LIMIT = 60 * 1024 * 1024


def dot(a, b):
    return jnp.dot(a, b, preferred_element_type=f32)


def dot_nt(a, b):
    return lax.dot_general(a, b, (((1,), (1,)), ((), ())), preferred_element_type=f32)


def permutation(to_wire):
    size = BLOCK * CHUNKS
    wire = lax.broadcasted_iota(jnp.int32, (size, size), 0 if to_wire else 1)
    held = lax.broadcasted_iota(jnp.int32, (size, size), 1 if to_wire else 0)
    return jnp.where((wire & (CHUNKS - 1)) * BLOCK + wire // CHUNKS == held, 1.0, 0.0).astype(bf16)


def to_wire(perm, rows, width):
    stacked = jnp.concatenate([rows[:, c * width : (c + 1) * width] for c in range(CHUNKS)], axis=0)
    return dot(perm, stacked).astype(bf16)


def route_kernel(role_ref, own_ref, partner_ref, expand_ref, target_ref, p_ref, pt_ref, gate_ref, hi_ref, lo_ref):
    experts = expand_ref.shape[1]
    rows = own_ref.shape[1]
    named = lax.broadcasted_iota(jnp.int32, (experts, rows), 0) + role_ref[0] * experts
    named = named.astype(f32)
    before = lax.broadcasted_iota(jnp.int32, (rows, rows), 0)
    after = lax.broadcasted_iota(jnp.int32, (rows, rows), 1)
    strict = jnp.where(before < after, 1.0, 0.0).astype(bf16)
    ranks, gates = [], []
    for ref in (own_ref, partner_ref):
        top = ref.shape[0] // 2
        uses = jnp.zeros((experts, rows), f32)
        gate = jnp.zeros((experts, rows), f32)
        for k in range(top):
            hit = named == ref[k : k + 1, :]
            uses = jnp.where(hit, 1.0, uses)
            gate = jnp.where(hit, ref[top + k : top + k + 1, :], gate)
        ranks.append(uses * (dot(uses.astype(bf16), strict) + 1.0))
        gates.append(gate)
    expand = expand_ref[...]
    rank = jnp.concatenate(ranks, axis=1).astype(bf16)
    gate = jnp.concatenate(gates, axis=1)
    chosen = dot(expand, rank) == target_ref[...].astype(f32)
    first = gate.astype(bf16)
    rest = gate - first.astype(f32)
    second = rest.astype(bf16)
    third = (rest - second.astype(f32)).astype(bf16)
    spread = dot(expand, first) + (dot(expand, second) + dot(expand, third))
    spread = jnp.where(chosen, spread, 0.0)
    one_hot = jnp.where(chosen, 1.0, 0.0)
    p_ref[...] = one_hot.astype(bf16)
    pt_ref[...] = jnp.transpose(one_hot).astype(bf16)
    gate_ref[...] = jnp.sum(spread, axis=1, keepdims=True)
    turned = jnp.transpose(spread)
    hi = turned.astype(bf16)
    hi_ref[...] = hi
    lo_ref[...] = (turned - hi.astype(f32)).astype(bf16)


def pack_normed_kernel(p_ref, own_ref, partner_ref, out_ref, normed_ref):
    rows, features = own_ref.shape

    @pl.when(pl.program_id(0) == 0)
    def _():
        for i, ref in enumerate((own_ref, partner_ref)):
            wide = ref[...].astype(f32)
            inv_rms = lax.rsqrt(jnp.mean(wide * wide, axis=1, keepdims=True) + epsilon)
            normed_ref[i * rows : (i + 1) * rows, :] = (wide * inv_rms).astype(bf16)

    gathered = dot(p_ref[...], normed_ref[...]).astype(bf16)
    out_ref[...] = to_wire(permutation(True), gathered, features // CHUNKS)


def pack_grad_kernel(p_ref, gate_ref, own_ref, partner_ref, out_ref):
    rows, features = own_ref.shape
    p = p_ref[...]
    gathered = dot(p[:, :rows], own_ref[...]) + dot(p[:, rows:], partner_ref[...])
    scaled = (gathered * gate_ref[...]).astype(bf16)
    out_ref[...] = to_wire(permutation(True), scaled, features // CHUNKS)


def pack(kernel, slots, rows, features, scratch, specs, args):
    wire = BLOCK * CHUNKS
    return pl.pallas_call(
        kernel,
        grid=(slots // BLOCK,),
        in_specs=specs,
        out_specs=pl.BlockSpec((wire, features // CHUNKS), lambda i: (i, 0)),
        out_shape=jax.ShapeDtypeStruct((slots * CHUNKS, features // CHUNKS), bf16),
        scratch_shapes=scratch,
        compiler_params=pltpu.CompilerParams(vmem_limit_bytes=VMEM_LIMIT),
        cost_estimate=pl.CostEstimate(
            flops=2 * slots * (2 * rows + wire) * features,
            bytes_accessed=2 * (2 * rows + slots) * features,
            transcendentals=0,
        ),
    )(*args)


def from_wire(wire_ref, out_ref):
    size, width = BLOCK * CHUNKS, wire_ref.shape[1]
    perm = permutation(False)

    def block(i, carry):
        turned = dot(perm, wire_ref[pl.ds(pl.multiple_of(i * size, size), size), :]).astype(bf16)
        at = pl.ds(pl.multiple_of(i * BLOCK, BLOCK), BLOCK)
        for c in range(CHUNKS):
            out_ref[at, c * width : (c + 1) * width] = turned[c * BLOCK : (c + 1) * BLOCK]
        return carry

    lax.fori_loop(0, out_ref.shape[0] // BLOCK, block, 0)


def put_on_wire(rows_ref, out_ref):
    size, width = BLOCK * CHUNKS, out_ref.shape[1]
    perm = permutation(True)

    def block(i, carry):
        at = pl.ds(pl.multiple_of(i * BLOCK, BLOCK), BLOCK)
        out_ref[pl.ds(pl.multiple_of(i * size, size), size), :] = to_wire(perm, rows_ref[at, :], width)
        return carry

    lax.fori_loop(0, rows_ref.shape[0] // BLOCK, block, 0)


def forward_kernel(wire_ref, gate_ref, up_ref, down_ref, out_ref, a_ref, b_ref, x_ref, product_ref):
    step = pl.program_id(0)
    tiles = product_ref.shape[0]
    width = out_ref.shape[1]

    @pl.when(step == 0)
    def _():
        from_wire(wire_ref, x_ref)

    @pl.when(step < tiles)
    def _():
        hidden_a = dot(x_ref[...], gate_ref[...])
        hidden_b = dot(x_ref[...], up_ref[...])
        a_ref[...] = hidden_a
        b_ref[...] = hidden_b
        product_ref[step] = (hidden_a * jax.nn.sigmoid(hidden_a) * hidden_b).astype(bf16)

    for c in range(CHUNKS):
        @pl.when(step == tiles + c)
        def _():
            product = jnp.concatenate([product_ref[n] for n in range(tiles)], axis=1)
            x_ref[:, c * width : (c + 1) * width] = dot(product, down_ref[...]).astype(bf16)

    @pl.when(step == tiles + CHUNKS - 1)
    def _():
        put_on_wire(x_ref, out_ref)


def backward_kernel(wire_ref, a_ref, b_ref, down_ref, gate_ref, up_ref, out_ref, x_ref, grad_ref):
    step = pl.program_id(0)
    tiles = grad_ref.shape[0] // 2
    width = out_ref.shape[1]

    @pl.when(step == 0)
    def _():
        from_wire(wire_ref, x_ref)

    @pl.when(step < tiles)
    def _():
        grad_act = dot_nt(x_ref[...], down_ref[...])
        hidden_a, hidden_b = a_ref[...], b_ref[...]
        sigmoid_a = jax.nn.sigmoid(hidden_a)
        slope = sigmoid_a * (1.0 + hidden_a * (1.0 - sigmoid_a))
        grad_ref[step] = (grad_act * hidden_b * slope).astype(bf16)
        grad_ref[tiles + step] = (grad_act * (hidden_a * sigmoid_a)).astype(bf16)

    for c in range(CHUNKS):
        @pl.when(step == tiles + c)
        def _():
            grad_a = jnp.concatenate([grad_ref[n] for n in range(tiles)], axis=1)
            grad_b = jnp.concatenate([grad_ref[tiles + n] for n in range(tiles)], axis=1)
            rows = dot_nt(grad_a, gate_ref[...]) + dot_nt(grad_b, up_ref[...])
            x_ref[:, c * width : (c + 1) * width] = rows.astype(bf16)

    @pl.when(step == tiles + CHUNKS - 1)
    def _():
        put_on_wire(x_ref, out_ref)


def expert_call(kernel, wire, weights, hidden, slots, features, units):
    tile = 256
    tiles = units // tile
    width = features // CHUNKS

    def early(i):
        return jnp.minimum(i, tiles - 1)

    def late(i):
        return jnp.maximum(i - tiles, 0)

    whole = pl.BlockSpec((slots * CHUNKS, width), lambda i: (0, 0))
    hidden_spec = pl.BlockSpec((slots, tile), lambda i: (0, early(i)))
    wire_shape = jax.ShapeDtypeStruct((slots * CHUNKS, width), bf16)
    if hidden is None:
        in_specs = [
            whole,
            pl.BlockSpec((features, tile), lambda i: (0, early(i))),
            pl.BlockSpec((features, tile), lambda i: (0, early(i))),
            pl.BlockSpec((units, width), lambda i: (0, late(i))),
        ]
        out_specs = [whole, hidden_spec, hidden_spec]
        out_shape = [wire_shape] + [jax.ShapeDtypeStruct((slots, units), f32)] * 2
        scratch = [pltpu.VMEM((slots, features), bf16), pltpu.VMEM((tiles, slots, tile), bf16)]
        args = (wire, *weights)
    else:
        in_specs = [
            whole,
            hidden_spec,
            hidden_spec,
            pl.BlockSpec((tile, features), lambda i: (early(i), 0)),
            pl.BlockSpec((width, units), lambda i: (late(i), 0)),
            pl.BlockSpec((width, units), lambda i: (late(i), 0)),
        ]
        out_specs, out_shape = whole, wire_shape
        scratch = [pltpu.VMEM((slots, features), bf16), pltpu.VMEM((2 * tiles, slots, tile), bf16)]
        args = (wire, *hidden, *weights)
    return pl.pallas_call(
        kernel,
        grid=(tiles + CHUNKS,),
        in_specs=in_specs,
        out_specs=out_specs,
        out_shape=out_shape,
        scratch_shapes=scratch,
        compiler_params=pltpu.CompilerParams(vmem_limit_bytes=VMEM_LIMIT),
        cost_estimate=pl.CostEstimate(
            flops=8 * slots * units * features,
            bytes_accessed=6 * units * features + 4 * slots * features + 8 * slots * units,
            transcendentals=slots * units,
        ),
    )(*args)


def combine_kernel(wire_ref, *refs):
    *matrix_refs, own_ref, partner_ref, rows_ref = refs
    step = pl.program_id(0)
    width = wire_ref.shape[1]
    turned = dot(permutation(False), wire_ref[...]).astype(bf16)
    at = pl.ds(pl.multiple_of(step * BLOCK, BLOCK), BLOCK)
    for c in range(CHUNKS):
        rows_ref[at, c * width : (c + 1) * width] = turned[c * BLOCK : (c + 1) * BLOCK]

    @pl.when(step == pl.num_programs(0) - 1)
    def _():
        count = own_ref.shape[0]
        rows = rows_ref[...]
        total = dot(matrix_refs[0][...], rows)
        for ref in matrix_refs[1:]:
            total = total + dot(ref[...], rows)
        own_ref[...] = total[:count].astype(own_ref.dtype)
        partner_ref[...] = total[count:].astype(partner_ref.dtype)


def combine(wire, matrices, slots, rows, features):
    size = BLOCK * CHUNKS
    matrix_spec = pl.BlockSpec((2 * rows, slots), lambda i: (0, 0))
    part_spec = pl.BlockSpec((rows, features), lambda i: (0, 0))
    return pl.pallas_call(
        combine_kernel,
        grid=(slots // BLOCK,),
        in_specs=[pl.BlockSpec((size, features // CHUNKS), lambda i: (i, 0))] + [matrix_spec] * len(matrices),
        out_specs=[part_spec, part_spec],
        out_shape=[jax.ShapeDtypeStruct((rows, features), f32)] * 2,
        scratch_shapes=[pltpu.VMEM((slots, features), bf16)],
        compiler_params=pltpu.CompilerParams(vmem_limit_bytes=VMEM_LIMIT),
        cost_estimate=pl.CostEstimate(
            flops=2 * slots * (2 * rows * len(matrices) + size) * features,
            bytes_accessed=2 * slots * features + 16 * rows * features,
            transcendentals=0,
        ),
    )(wire, *matrices)


def local(tokens, grad_out, routes, gates, gate_weight, up_weight, down_weight):
    rows, features = tokens.shape
    top = routes.shape[1]
    units = gate_weight.shape[2]
    chips = lax.axis_size("dev")
    cap = rows * top * 5 // (4 * chips * lax.axis_size("role"))
    per_chip = 2 * cap
    slots = chips * per_chip
    role = lax.axis_index("role").astype(jnp.int32).reshape(1)
    swap = [(0, 1), (1, 0)]

    def other(array):
        return lax.ppermute(array, "role", swap)

    route_info = jnp.concatenate([routes.astype(f32), gates], axis=1).T
    route_other = other(route_info)
    tokens_other = other(tokens)
    grad_other = other(grad_out)

    place = np.arange(slots)
    expand = (place[:, None] // per_chip == np.arange(chips)[None, :]).astype(np.float32)
    source, number = place % per_chip // cap, place % cap
    target = np.where(np.arange(2 * rows)[None, :] // rows == source[:, None], number[:, None] + 1, -1)
    vmem = pl.BlockSpec(memory_space=pltpu.VMEM)
    p, p_turned, slot_gate, gate_hi, gate_lo = pl.pallas_call(
        route_kernel,
        in_specs=[pl.BlockSpec(memory_space=pltpu.SMEM)] + [vmem] * 4,
        out_specs=[vmem] * 5,
        out_shape=[
            jax.ShapeDtypeStruct((slots, 2 * rows), bf16),
            jax.ShapeDtypeStruct((2 * rows, slots), bf16),
            jax.ShapeDtypeStruct((slots, 1), f32),
            jax.ShapeDtypeStruct((2 * rows, slots), bf16),
            jax.ShapeDtypeStruct((2 * rows, slots), bf16),
        ],
    )(role, route_info, route_other, jnp.asarray(expand, bf16), jnp.asarray(target, bf16))

    p_spec = pl.BlockSpec((BLOCK, 2 * rows), lambda i: (i, 0))
    slot_spec = pl.BlockSpec((BLOCK, 1), lambda i: (i, 0))
    rows_spec = pl.BlockSpec((rows, features), lambda i: (0, 0))
    normed_wire = pack(
        pack_normed_kernel, slots, rows, features, [pltpu.VMEM((2 * rows, features), bf16)],
        [p_spec, rows_spec, rows_spec], (p, tokens, tokens_other),
    )
    grad_wire = pack(
        pack_grad_kernel, slots, rows, features, [],
        [p_spec, slot_spec, rows_spec, rows_spec], (p, slot_gate, grad_out, grad_other),
    )

    def exchange(wire):
        parts = wire.reshape(chips, per_chip * CHUNKS, features // CHUNKS)
        parts = lax.all_to_all(parts, "dev", split_axis=0, concat_axis=0, tiled=True)
        return parts.reshape(wire.shape)

    gate_local, up_local, down_local = gate_weight[0], up_weight[0], down_weight[0]
    normed_in = exchange(normed_wire)
    grad_in_wire = exchange(grad_wire)
    out_wire, hidden_a, hidden_b = expert_call(
        forward_kernel, normed_in, (gate_local, up_local, down_local), None, slots, features, units
    )
    out_back = exchange(out_wire)
    rows_wire = expert_call(
        backward_kernel, grad_in_wire, (down_local, gate_local, up_local), (hidden_a, hidden_b), slots, features, units
    )
    rows_back = exchange(rows_wire)

    out_own, out_partner = combine(out_back, (gate_hi, gate_lo), slots, rows, features)
    tokens_wide = tokens.astype(f32)
    layer_out = (tokens_wide + (out_own + other(out_partner))).astype(bf16)

    grad_own, grad_partner = combine(rows_back, (p_turned,), slots, rows, features)
    grad_normed = grad_own + other(grad_partner)
    inv_rms = lax.rsqrt(jnp.mean(tokens_wide * tokens_wide, axis=1, keepdims=True) + epsilon)
    projected = jnp.mean(grad_normed * tokens_wide, axis=1, keepdims=True)
    grad_in = grad_out.astype(f32) + inv_rms * grad_normed - tokens_wide * inv_rms**3 * projected
    return (layer_out, grad_in.astype(bf16))


def solution(mesh):
    split = P(("role", "dev"), None)
    split_weight = P(("role", "dev"), None, None)
    in_specs = (split, split, split, split, split_weight, split_weight, split_weight)
    return jax.shard_map(local, mesh=mesh, in_specs=in_specs, out_specs=(split, split), check_vma=False)
```

```python
import functools

import jax
import jax.numpy as jnp
from jax import lax
from jax.experimental import pallas as pl
from jax.experimental.pallas import tpu as pltpu
from jax.sharding import PartitionSpec as P

epsilon = 1e-06
bf16, f32 = jnp.bfloat16, jnp.float32
CHUNKS = 4
BLOCK = 64
PACK = 320
VMEM_LIMIT = 60 * 1024 * 1024
SMALL_LIMIT = 40 * 1024 * 1024


def dot(a, b):
    return jnp.dot(a, b, preferred_element_type=f32)


def dot_nt(a, b):
    return lax.dot_general(a, b, (((1,), (1,)), ((), ())), preferred_element_type=f32)


def permutation(to_wire):
    size = BLOCK * CHUNKS
    wire = lax.broadcasted_iota(jnp.int32, (size, size), 0 if to_wire else 1)
    held = lax.broadcasted_iota(jnp.int32, (size, size), 1 if to_wire else 0)
    return jnp.where((wire & (CHUNKS - 1)) * BLOCK + wire // CHUNKS == held, 1.0, 0.0).astype(bf16)


def to_wire(perm, rows, width):
    stacked = jnp.concatenate([rows[:, c * width : (c + 1) * width] for c in range(CHUNKS)], axis=0)
    return dot(perm, stacked).astype(bf16)


def slot_tables(chips, slots, rows):
    per_chip = slots // chips
    cap = per_chip // 2
    slot = lax.broadcasted_iota(jnp.int32, (slots, chips), 0)
    first = lax.broadcasted_iota(jnp.int32, (slots, chips), 1) * per_chip
    expand = jnp.where((slot >= first) & (slot < first + per_chip), 1.0, 0.0)
    place = slot[:, :1].astype(f32) - jnp.sum(jnp.where(expand > 0.0, first.astype(f32), 0.0), axis=1, keepdims=True)
    partner = place >= cap
    rank = jnp.where(partner, place - cap, place) + 1.0
    lane = lax.broadcasted_iota(jnp.int32, (slots, 2 * rows), 1).astype(f32)
    side = jnp.where(partner, 1.0, 0.0)
    target = jnp.where(jnp.where(lane >= rows, 1.0, 0.0) == side, rank, -1.0)
    return expand.astype(bf16), target


def chosen_slots(role, sides, chips, slots):
    top, rows = sides[0][0].shape
    expand, target = slot_tables(chips, slots, rows)
    named = lax.broadcasted_iota(jnp.int32, (chips, rows), 0) + role * chips
    before = lax.broadcasted_iota(jnp.int32, (rows, rows), 0)
    after = lax.broadcasted_iota(jnp.int32, (rows, rows), 1)
    strict = jnp.where(before < after, 1.0, 0.0).astype(bf16)
    ranks, gates = [], []
    for route_ref, gate_ref in sides:
        uses = jnp.zeros((chips, rows), f32)
        gate = jnp.zeros((chips, rows), f32)
        for k in range(top):
            hit = named == route_ref[k : k + 1, :]
            uses = jnp.where(hit, 1.0, uses)
            gate = jnp.where(hit, gate_ref[k : k + 1, :], gate)
        ranks.append(uses * (dot(uses.astype(bf16), strict) + 1.0))
        gates.append(gate)
    rank = jnp.concatenate(ranks, axis=1).astype(bf16)
    gate = jnp.concatenate(gates, axis=1)
    chosen = dot(expand, rank) == target
    first = gate.astype(bf16)
    rest = gate - first.astype(f32)
    second = rest.astype(bf16)
    third = (rest - second.astype(f32)).astype(bf16)
    spread = dot(expand, first) + (dot(expand, second) + dot(expand, third))
    return jnp.where(chosen, 1.0, 0.0), jnp.where(chosen, spread, 0.0)


def wire_blocks(out_ref, perm, rows):
    size, width = BLOCK * CHUNKS, out_ref.shape[1]
    for i in range(rows.shape[0] // BLOCK):
        out_ref[i * size : (i + 1) * size, :] = to_wire(perm, rows[i * BLOCK : (i + 1) * BLOCK], width)


def pack_kernel(
    chips, role_ref, route_ref, route_other_ref, gate_ref, gate_other_ref,
    tokens_ref, tokens_other_ref, grad_ref, grad_other_ref,
    normed_wire_ref, grad_wire_ref, pt_ref, hi_ref, lo_ref,
    normed_ref, p_ref, slot_gate_ref, perm_ref,
):
    rows = tokens_ref.shape[0]
    slots = p_ref.shape[0]
    step = pl.program_id(0)
    half = slots // PACK

    @pl.when(step == 0)
    def _():
        perm_ref[...] = permutation(True)
        sides = ((route_ref, gate_ref), (route_other_ref, gate_other_ref))
        one_hot, spread = chosen_slots(role_ref[0], sides, chips, slots)
        p_ref[...] = one_hot.astype(bf16)
        slot_gate_ref[...] = jnp.sum(spread, axis=1, keepdims=True)
        pt_ref[...] = jnp.transpose(one_hot).astype(bf16)
        turned = jnp.transpose(spread)
        hi = turned.astype(bf16)
        hi_ref[...] = hi
        lo_ref[...] = (turned - hi.astype(f32)).astype(bf16)
        for i, ref in enumerate((tokens_ref, tokens_other_ref)):
            wide = ref[...].astype(f32)
            inv_rms = lax.rsqrt(jnp.mean(wide * wide, axis=1, keepdims=True) + epsilon)
            normed_ref[i * rows : (i + 1) * rows, :] = (wide * inv_rms).astype(bf16)

    at = pl.ds(pl.multiple_of(lax.rem(step, half) * PACK, PACK), PACK)

    @pl.when(step < half)
    def _():
        wire_blocks(normed_wire_ref, perm_ref[...], dot(p_ref[at, :], normed_ref[...]).astype(bf16))

    @pl.when(step >= half)
    def _():
        p = p_ref[at, :]
        gathered = dot(p[:, :rows], grad_ref[...]) + dot(p[:, rows:], grad_other_ref[...])
        wire_blocks(grad_wire_ref, perm_ref[...], (gathered * slot_gate_ref[at, :]).astype(bf16))


def pack(role, routes, gates, tokens, grads, chips, slots):
    rows, features = tokens[0].shape
    top = routes[0].shape[0]
    half = slots // PACK
    width = features // CHUNKS

    def fixed(*shape):
        return pl.BlockSpec(shape, lambda i: (0,) * len(shape))

    lane_spec, rows_spec, turned_spec = fixed(top, rows), fixed(rows, features), fixed(2 * rows, slots)
    wire_shape = jax.ShapeDtypeStruct((slots * CHUNKS, width), bf16)
    turned_shape = jax.ShapeDtypeStruct((2 * rows, slots), bf16)
    return pl.pallas_call(
        functools.partial(pack_kernel, chips),
        grid=(2 * half,),
        in_specs=[pl.BlockSpec(memory_space=pltpu.SMEM)] + [lane_spec] * 4 + [rows_spec] * 4,
        out_specs=[
            pl.BlockSpec((PACK * CHUNKS, width), lambda i: (jnp.minimum(i, half - 1), 0)),
            pl.BlockSpec((PACK * CHUNKS, width), lambda i: (jnp.maximum(i - half, 0), 0)),
            turned_spec, turned_spec, turned_spec,
        ],
        out_shape=[wire_shape, wire_shape, turned_shape, turned_shape, turned_shape],
        scratch_shapes=[
            pltpu.VMEM((2 * rows, features), bf16),
            pltpu.VMEM((slots, 2 * rows), bf16),
            pltpu.VMEM((slots, 1), f32),
            pltpu.VMEM((BLOCK * CHUNKS, BLOCK * CHUNKS), bf16),
        ],
        compiler_params=pltpu.CompilerParams(vmem_limit_bytes=VMEM_LIMIT),
        cost_estimate=pl.CostEstimate(
            flops=4 * slots * (2 * rows + BLOCK * CHUNKS) * features,
            bytes_accessed=4 * (2 * rows + slots) * features,
            transcendentals=0,
        ),
    )(role, *routes, *gates, tokens[0], tokens[1], grads[0], grads[1])


def from_wire(wire_ref, out_ref):
    size, width = BLOCK * CHUNKS, wire_ref.shape[1]
    perm = permutation(False)

    def block(i, carry):
        turned = dot(perm, wire_ref[pl.ds(pl.multiple_of(i * size, size), size), :]).astype(bf16)
        at = pl.ds(pl.multiple_of(i * BLOCK, BLOCK), BLOCK)
        for c in range(CHUNKS):
            out_ref[at, c * width : (c + 1) * width] = turned[c * BLOCK : (c + 1) * BLOCK]
        return carry

    lax.fori_loop(0, out_ref.shape[0] // BLOCK, block, 0)


def put_on_wire(rows_ref, out_ref):
    size, width = BLOCK * CHUNKS, out_ref.shape[1]
    perm = permutation(True)

    def block(i, carry):
        at = pl.ds(pl.multiple_of(i * BLOCK, BLOCK), BLOCK)
        out_ref[pl.ds(pl.multiple_of(i * size, size), size), :] = to_wire(perm, rows_ref[at, :], width)
        return carry

    lax.fori_loop(0, rows_ref.shape[0] // BLOCK, block, 0)


def forward_kernel(wire_ref, gate_ref, up_ref, down_ref, out_ref, a_ref, b_ref, x_ref, product_ref):
    step = pl.program_id(0)
    tiles = product_ref.shape[0]
    width = out_ref.shape[1]

    @pl.when(step == 0)
    def _():
        from_wire(wire_ref, x_ref)

    @pl.when(step < tiles)
    def _():
        hidden_a = dot(x_ref[...], gate_ref[...])
        hidden_b = dot(x_ref[...], up_ref[...])
        a_ref[...] = hidden_a
        b_ref[...] = hidden_b
        product_ref[step] = (hidden_a * jax.nn.sigmoid(hidden_a) * hidden_b).astype(bf16)

    for c in range(CHUNKS):
        @pl.when(step == tiles + c)
        def _():
            product = jnp.concatenate([product_ref[n] for n in range(tiles)], axis=1)
            x_ref[:, c * width : (c + 1) * width] = dot(product, down_ref[...]).astype(bf16)

    @pl.when(step == tiles + CHUNKS - 1)
    def _():
        put_on_wire(x_ref, out_ref)


def backward_kernel(wire_ref, a_ref, b_ref, down_ref, gate_ref, up_ref, out_ref, x_ref, grad_ref):
    step = pl.program_id(0)
    tiles = grad_ref.shape[0] // 2
    width = out_ref.shape[1]

    @pl.when(step == 0)
    def _():
        from_wire(wire_ref, x_ref)

    @pl.when(step < tiles)
    def _():
        grad_act = dot_nt(x_ref[...], down_ref[...])
        hidden_a, hidden_b = a_ref[...], b_ref[...]
        sigmoid_a = jax.nn.sigmoid(hidden_a)
        slope = sigmoid_a * (1.0 + hidden_a * (1.0 - sigmoid_a))
        grad_ref[step] = (grad_act * hidden_b * slope).astype(bf16)
        grad_ref[tiles + step] = (grad_act * (hidden_a * sigmoid_a)).astype(bf16)

    for c in range(CHUNKS):
        @pl.when(step == tiles + c)
        def _():
            grad_a = jnp.concatenate([grad_ref[n] for n in range(tiles)], axis=1)
            grad_b = jnp.concatenate([grad_ref[tiles + n] for n in range(tiles)], axis=1)
            rows = dot_nt(grad_a, gate_ref[...]) + dot_nt(grad_b, up_ref[...])
            x_ref[:, c * width : (c + 1) * width] = rows.astype(bf16)

    @pl.when(step == tiles + CHUNKS - 1)
    def _():
        put_on_wire(x_ref, out_ref)


def expert_call(kernel, wire, weights, hidden, slots, features, units):
    tile = 256
    tiles = units // tile
    width = features // CHUNKS

    def early(i):
        return jnp.minimum(i, tiles - 1)

    def late(i):
        return jnp.maximum(i - tiles, 0)

    whole = pl.BlockSpec((slots * CHUNKS, width), lambda i: (0, 0))
    hidden_spec = pl.BlockSpec((slots, tile), lambda i: (0, early(i)))
    wire_shape = jax.ShapeDtypeStruct((slots * CHUNKS, width), bf16)
    if hidden is None:
        in_specs = [
            whole,
            pl.BlockSpec((features, tile), lambda i: (0, early(i))),
            pl.BlockSpec((features, tile), lambda i: (0, early(i))),
            pl.BlockSpec((units, width), lambda i: (0, late(i))),
        ]
        out_specs = [whole, hidden_spec, hidden_spec]
        out_shape = [wire_shape] + [jax.ShapeDtypeStruct((slots, units), f32)] * 2
        scratch = [pltpu.VMEM((slots, features), bf16), pltpu.VMEM((tiles, slots, tile), bf16)]
        args = (wire, *weights)
    else:
        in_specs = [
            whole,
            hidden_spec,
            hidden_spec,
            pl.BlockSpec((tile, features), lambda i: (early(i), 0)),
            pl.BlockSpec((width, units), lambda i: (late(i), 0)),
            pl.BlockSpec((width, units), lambda i: (late(i), 0)),
        ]
        out_specs, out_shape = whole, wire_shape
        scratch = [pltpu.VMEM((slots, features), bf16), pltpu.VMEM((2 * tiles, slots, tile), bf16)]
        args = (wire, *hidden, *weights)
    return pl.pallas_call(
        kernel,
        grid=(tiles + CHUNKS,),
        in_specs=in_specs,
        out_specs=out_specs,
        out_shape=out_shape,
        scratch_shapes=scratch,
        compiler_params=pltpu.CompilerParams(vmem_limit_bytes=VMEM_LIMIT),
        cost_estimate=pl.CostEstimate(
            flops=8 * slots * units * features,
            bytes_accessed=6 * units * features + 4 * slots * features + 8 * slots * units,
            transcendentals=slots * units,
        ),
    )(*args)


def combine_kernel(
    out_wire_ref, grad_wire_ref, pt_ref, hi_ref, lo_ref, out_own_ref, grad_own_ref, partner_ref,
    out_rows_ref, grad_rows_ref, perm_ref,
):
    step = pl.program_id(0)
    size, width = BLOCK * CHUNKS, out_wire_ref.shape[1]

    @pl.when(step == 0)
    def _():
        perm_ref[...] = permutation(False)

    perm = perm_ref[...]
    for wire_ref, rows_ref in ((out_wire_ref, out_rows_ref), (grad_wire_ref, grad_rows_ref)):
        for i in range(PACK // BLOCK):
            turned = dot(perm, wire_ref[i * size : (i + 1) * size, :]).astype(bf16)
            at = pl.ds(pl.multiple_of(step * PACK + i * BLOCK, BLOCK), BLOCK)
            for c in range(CHUNKS):
                rows_ref[at, c * width : (c + 1) * width] = turned[c * BLOCK : (c + 1) * BLOCK]

    @pl.when(step == pl.num_programs(0) - 1)
    def _():
        count = out_own_ref.shape[0]
        for c in range(CHUNKS):
            at = slice(c * width, (c + 1) * width)
            rows = out_rows_ref[:, at]
            total = dot(hi_ref[...], rows) + dot(lo_ref[...], rows)
            out_own_ref[:, at] = total[:count]
            partner_ref[0, :, at] = total[count:].astype(bf16)
            total = dot(pt_ref[...], grad_rows_ref[:, at])
            grad_own_ref[:, at] = total[:count]
            partner_ref[1, :, at] = total[count:].astype(bf16)


def combine(out_wire, grad_wire, matrices, slots, rows, features):
    size, width = BLOCK * CHUNKS, features // CHUNKS
    wire_spec = pl.BlockSpec((PACK * CHUNKS, width), lambda i: (i, 0))
    matrix_spec = pl.BlockSpec((2 * rows, slots), lambda i: (0, 0))
    part_spec = pl.BlockSpec((rows, features), lambda i: (0, 0))
    return pl.pallas_call(
        combine_kernel,
        grid=(slots // PACK,),
        in_specs=[wire_spec] * 2 + [matrix_spec] * 3,
        out_specs=[part_spec, part_spec, pl.BlockSpec((2, rows, features), lambda i: (0, 0, 0))],
        out_shape=[
            jax.ShapeDtypeStruct((rows, features), f32),
            jax.ShapeDtypeStruct((rows, features), f32),
            jax.ShapeDtypeStruct((2, rows, features), bf16),
        ],
        scratch_shapes=[
            pltpu.VMEM((slots, features), bf16),
            pltpu.VMEM((slots, features), bf16),
            pltpu.VMEM((size, size), bf16),
        ],
        compiler_params=pltpu.CompilerParams(vmem_limit_bytes=SMALL_LIMIT),
        cost_estimate=pl.CostEstimate(
            flops=4 * slots * (3 * rows + size) * features,
            bytes_accessed=4 * slots * features + 16 * rows * features,
            transcendentals=0,
        ),
    )(out_wire, grad_wire, *matrices)


def local(tokens, grad_out, routes, gates, gate_weight, up_weight, down_weight):
    rows, features = tokens.shape
    top = routes.shape[1]
    units = gate_weight.shape[2]
    chips = lax.axis_size("dev")
    cap = rows * top * 5 // (4 * chips * lax.axis_size("role"))
    per_chip = 2 * cap
    slots = chips * per_chip
    role = lax.axis_index("role").astype(jnp.int32).reshape(1)
    swap = [(0, 1), (1, 0)]

    def other(array):
        return lax.ppermute(array, "role", swap)

    route_lanes, gate_lanes = routes.T, gates.T
    normed_wire, grad_wire, *matrices = pack(
        role,
        (route_lanes, other(route_lanes)),
        (gate_lanes, other(gate_lanes)),
        (tokens, other(tokens)),
        (grad_out, other(grad_out)),
        chips,
        slots,
    )

    def exchange(wire):
        parts = wire.reshape(chips, per_chip * CHUNKS, features // CHUNKS)
        parts = lax.all_to_all(parts, "dev", split_axis=0, concat_axis=0, tiled=True)
        return parts.reshape(wire.shape)

    gate_local, up_local, down_local = gate_weight[0], up_weight[0], down_weight[0]
    normed_in = exchange(normed_wire)
    grad_in_wire = exchange(grad_wire)
    out_wire, hidden_a, hidden_b = expert_call(
        forward_kernel, normed_in, (gate_local, up_local, down_local), None, slots, features, units
    )
    out_back = exchange(out_wire)
    rows_wire = expert_call(
        backward_kernel, grad_in_wire, (down_local, gate_local, up_local), (hidden_a, hidden_b), slots, features, units
    )
    rows_wire, _ = lax.optimization_barrier((rows_wire, out_back))
    rows_back = exchange(rows_wire)

    out_own, grad_own, partner = combine(out_back, rows_back, matrices, slots, rows, features)
    received = other(partner).astype(f32)
    tokens_wide = tokens.astype(f32)
    layer_out = (tokens_wide + (out_own + received[0])).astype(bf16)
    grad_normed = grad_own + received[1]
    inv_rms = lax.rsqrt(jnp.mean(tokens_wide * tokens_wide, axis=1, keepdims=True) + epsilon)
    projected = jnp.mean(grad_normed * tokens_wide, axis=1, keepdims=True)
    grad_in = grad_out.astype(f32) + inv_rms * grad_normed - tokens_wide * inv_rms**3 * projected
    return (layer_out, grad_in.astype(bf16))


def solution(mesh):
    split = P(("role", "dev"), None)
    split_weight = P(("role", "dev"), None, None)
    in_specs = (split, split, split, split, split_weight, split_weight, split_weight)
    return jax.shard_map(local, mesh=mesh, in_specs=in_specs, out_specs=(split, split), check_vma=False)
```

```python
import functools
import math

import jax
import jax.numpy as jnp
from jax import lax
from jax.experimental import pallas as pl
from jax.experimental.pallas import tpu as pltpu
from jax.sharding import PartitionSpec as P

epsilon = 1e-06
bf16, f32 = jnp.bfloat16, jnp.float32
CHUNKS = 4
BLOCK = 64
EARLY = 6
PER_CHIP = 10
AHEAD = 5 * 1024 * 1024
FORWARD_TILE, BACKWARD_TILE = 256, 512
GROUP = 16
VMEM_LIMIT = 60 * 1024 * 1024
SMALL_LIMIT = 40 * 1024 * 1024


def dot(a, b):
    return jnp.dot(a, b, preferred_element_type=f32)


def dot_nt(a, b):
    return lax.dot_general(a, b, (((1,), (1,)), ((), ())), preferred_element_type=f32)


LATE = PER_CHIP - EARLY
UNITS = PER_CHIP + EARLY
SIDE = BLOCK // UNITS
TEN_EARLY, TEN_LATE = SIDE * EARLY, SIDE * LATE


def permutation(to_wire, mixed):
    size = BLOCK * CHUNKS
    wire = lax.broadcasted_iota(jnp.int32, (size, size), 0 if to_wire else 1)
    held = lax.broadcasted_iota(jnp.int32, (size, size), 1 if to_wire else 0)
    unit = lax.shift_right_logical(wire, 2)
    if mixed:
        chip, part = lax.shift_right_logical(unit, 4), unit & (UNITS - 1)
        six = TEN_EARLY + TEN_LATE + chip * EARLY + part - PER_CHIP
        late = TEN_EARLY + chip * LATE + part - EARLY
        unit = jnp.where(part < EARLY, chip * EARLY + part, jnp.where(part < PER_CHIP, late, six))
    return jnp.where((wire & (CHUNKS - 1)) * BLOCK + unit == held, 1.0, 0.0).astype(bf16)


def to_wire(perm, rows, width):
    stacked = jnp.concatenate([rows[:, c * width : (c + 1) * width] for c in range(CHUNKS)], axis=0)
    return dot(perm, stacked).astype(bf16)


def mixed_to_wire(out_ref, base, perm, ten_early, ten_late, six, width):
    size = BLOCK * CHUNKS
    for j in range(six.shape[0] // TEN_EARLY):
        rows = jnp.concatenate(
            [
                ten_early[j * TEN_EARLY : (j + 1) * TEN_EARLY],
                ten_late[j * TEN_LATE : (j + 1) * TEN_LATE],
                six[j * TEN_EARLY : (j + 1) * TEN_EARLY],
            ],
            axis=0,
        ).astype(bf16)
        out_ref[pl.ds(base + j * size, size), :] = to_wire(perm, rows, width)


def mixed_from_wire(wire_ref, base, perm, pair, early, ten_ref, six_ref):
    size, width = BLOCK * CHUNKS, wire_ref.shape[1]
    turned = [dot(perm, wire_ref[pl.ds(base + j * size, size), :]) for j in range(2)]
    edges = (0, TEN_EARLY, TEN_EARLY + TEN_LATE, BLOCK)
    places = (
        (ten_ref, pair * 2 * TEN_EARLY, 2 * TEN_EARLY),
        (ten_ref, early + pair * 2 * TEN_LATE, 2 * TEN_LATE),
        (six_ref, pair * 2 * TEN_EARLY, 2 * TEN_EARLY),
    )
    for n, (ref, start, count) in enumerate(places):
        at = pl.ds(pl.multiple_of(start, 16), count)
        for c in range(CHUNKS):
            rows = [t[c * BLOCK + edges[n] : c * BLOCK + edges[n + 1]] for t in turned]
            ref[at, c * width : (c + 1) * width] = jnp.concatenate(rows, axis=0).astype(bf16)


def plain_from_wire(wire_ref, base, perm, ref, start):
    size, width = BLOCK * CHUNKS, wire_ref.shape[1]
    turned = dot(perm, wire_ref[pl.ds(base, size), :]).astype(bf16)
    at = pl.ds(pl.multiple_of(start, 16), BLOCK)
    for c in range(CHUNKS):
        ref[at, c * width : (c + 1) * width] = turned[c * BLOCK : (c + 1) * BLOCK]


def slot_tables(chips, slots, rows):
    early = chips * EARLY
    cap = PER_CHIP // 2
    slot = lax.broadcasted_iota(jnp.int32, (slots, chips), 0)
    chip = lax.broadcasted_iota(jnp.int32, (slots, chips), 1)
    first = jnp.where(slot < early, chip * EARLY, early + chip * LATE)
    count = jnp.where(slot < early, EARLY, LATE)
    expand = jnp.where((slot >= first) & (slot < first + count), 1.0, 0.0)
    base = jnp.where(slot < early, first, first - EARLY).astype(f32)
    place = slot[:, :1].astype(f32) - jnp.sum(expand * base, axis=1, keepdims=True)
    partner = place >= cap
    rank = jnp.where(partner, place - cap, place) + 1.0
    lane = lax.broadcasted_iota(jnp.int32, (slots, 2 * rows), 1).astype(f32)
    side = jnp.where(partner, 1.0, 0.0)
    target = jnp.where(jnp.where(lane >= rows, 1.0, 0.0) == side, rank, -1.0)
    return expand.astype(bf16), target


def chosen_slots(role, sides, chips, slots):
    top, rows = sides[0][0].shape
    expand, target = slot_tables(chips, slots, rows)
    named = lax.broadcasted_iota(jnp.int32, (chips, rows), 0) + role * chips
    before = lax.broadcasted_iota(jnp.int32, (rows, rows), 0)
    after = lax.broadcasted_iota(jnp.int32, (rows, rows), 1)
    strict = jnp.where(before < after, 1.0, 0.0).astype(bf16)
    ranks, gates = [], []
    for route_ref, gate_ref in sides:
        uses = jnp.zeros((chips, rows), f32)
        gate = jnp.zeros((chips, rows), f32)
        for k in range(top):
            hit = named == route_ref[k : k + 1, :]
            uses = jnp.where(hit, 1.0, uses)
            gate = jnp.where(hit, gate_ref[k : k + 1, :], gate)
        ranks.append(uses * (dot(uses.astype(bf16), strict) + 1.0))
        gates.append(gate)
    rank = jnp.concatenate(ranks, axis=1).astype(bf16)
    gate = jnp.concatenate(gates, axis=1)
    chosen = dot(expand, rank) == target
    first = gate.astype(bf16)
    rest = gate - first.astype(f32)
    second = rest.astype(bf16)
    third = (rest - second.astype(f32)).astype(bf16)
    spread = dot(expand, first) + (dot(expand, second) + dot(expand, third))
    return jnp.where(chosen, 1.0, 0.0), jnp.where(chosen, spread, 0.0)


def route_kernel(
    chips, role_ref, route_ref, route_other_ref, gate_ref, gate_other_ref, p_ref, slot_gate_ref, pt_ref, hi_ref, lo_ref
):
    sides = ((route_ref, gate_ref), (route_other_ref, gate_other_ref))
    one_hot, spread = chosen_slots(role_ref[0], sides, chips, p_ref.shape[0])
    p_ref[...] = one_hot.astype(bf16)
    slot_gate_ref[...] = jnp.sum(spread, axis=1, keepdims=True)
    pt_ref[...] = jnp.transpose(one_hot).astype(bf16)
    turned = jnp.transpose(spread)
    hi = turned.astype(bf16)
    hi_ref[...] = hi
    lo_ref[...] = (turned - hi.astype(f32)).astype(bf16)


def route(role, routes, gates, chips, slots):
    rows = routes[0].shape[1]
    vmem = pl.BlockSpec(memory_space=pltpu.VMEM)
    turned_shape = jax.ShapeDtypeStruct((2 * rows, slots), bf16)
    return pl.pallas_call(
        functools.partial(route_kernel, chips),
        in_specs=[pl.BlockSpec(memory_space=pltpu.SMEM)] + [vmem] * 4,
        out_specs=[vmem] * 5,
        out_shape=[
            jax.ShapeDtypeStruct((slots, 2 * rows), bf16),
            jax.ShapeDtypeStruct((slots, 1), f32),
            turned_shape, turned_shape, turned_shape,
        ],
        compiler_params=pltpu.CompilerParams(vmem_limit_bytes=VMEM_LIMIT),
        cost_estimate=pl.CostEstimate(
            flops=8 * slots * rows * chips, bytes_accessed=12 * slots * rows, transcendentals=0
        ),
    )(role, *routes, *gates)


def pack_kernel(
    p_early_ref, p_late_ref, gate_early_ref, gate_late_ref, tokens_ref, tokens_other_ref, grad_ref, grad_other_ref,
    large_ref, small_ref, normed_ref, mixed_ref, plain_ref,
):
    rows = tokens_ref.shape[0]
    width = large_ref.shape[1]

    @pl.when(pl.program_id(0) == 0)
    def _():
        mixed_ref[...] = permutation(True, True)
        plain_ref[...] = permutation(True, False)
        for i, ref in enumerate((tokens_ref, tokens_other_ref)):
            wide = ref[...].astype(f32)
            inv_rms = lax.rsqrt(jnp.mean(wide * wide, axis=1, keepdims=True) + epsilon)
            normed_ref[i * rows : (i + 1) * rows, :] = (wide * inv_rms).astype(bf16)

    early = p_early_ref.shape[0]
    p = jnp.concatenate([p_early_ref[...], p_late_ref[...]], axis=0)
    gate = jnp.concatenate([gate_early_ref[...], gate_late_ref[...]], axis=0)
    normed = dot(p, normed_ref[...])
    scaled = (dot(p[:, :rows], grad_ref[...]) + dot(p[:, rows:], grad_other_ref[...])) * gate
    mixed_to_wire(large_ref, 0, mixed_ref[...], normed[:early], normed[early:], scaled[:early], width)
    small_ref[...] = to_wire(plain_ref[...], scaled[early:].astype(bf16), width)


def pack(p, slot_gate, tokens, grads, chips, slots):
    rows, features = tokens[0].shape
    width = features // CHUNKS
    late = chips * EARLY // (GROUP * LATE)
    size = BLOCK * CHUNKS
    rows_spec = pl.BlockSpec((rows, features), lambda i: (0, 0))
    large, small = GROUP * UNITS * CHUNKS, GROUP * LATE * CHUNKS
    steps = chips // GROUP
    return pl.pallas_call(
        pack_kernel,
        grid=(steps,),
        in_specs=[
            pl.BlockSpec((GROUP * EARLY, 2 * rows), lambda i: (i, 0)),
            pl.BlockSpec((GROUP * LATE, 2 * rows), lambda i: (late + i, 0)),
            pl.BlockSpec((GROUP * EARLY, 1), lambda i: (i, 0)),
            pl.BlockSpec((GROUP * LATE, 1), lambda i: (late + i, 0)),
        ]
        + [rows_spec] * 4,
        out_specs=[
            pl.BlockSpec((large, width), lambda i: (i, 0)),
            pl.BlockSpec((small, width), lambda i: (i, 0)),
        ],
        out_shape=[
            jax.ShapeDtypeStruct((steps * large, width), bf16),
            jax.ShapeDtypeStruct((steps * small, width), bf16),
        ],
        scratch_shapes=[
            pltpu.VMEM((2 * rows, features), bf16),
            pltpu.VMEM((size, size), bf16),
            pltpu.VMEM((size, size), bf16),
        ],
        compiler_params=pltpu.CompilerParams(vmem_limit_bytes=VMEM_LIMIT),
        cost_estimate=pl.CostEstimate(
            flops=4 * slots * (2 * rows + size) * features,
            bytes_accessed=4 * (2 * rows + slots) * features,
            transcendentals=0,
        ),
    )(p, p, slot_gate, slot_gate, *tokens, *grads)


class Copies:
    def __init__(self, sems):
        self.sems, self.made = sems, 0
        self.queue, self.flying, self.flying_bytes = [], [], 0

    def start(self, source, target):
        copy = pltpu.make_async_copy(source, target, self.sems.at[self.made])
        self.made += 1
        copy.start()
        return copy

    def add(self, source, target):
        self.queue.append((source, target, math.prod(target.shape) * target.dtype.itemsize))

    def fill(self):
        while self.queue and self.flying_bytes < AHEAD:
            source, target, size = self.queue.pop(0)
            self.flying.append((self.start(source, target), size))
            self.flying_bytes += size

    def take(self, count=1):
        for _ in range(count):
            self.fill()
            copy, size = self.flying.pop(0)
            copy.wait()
            self.flying_bytes -= size
        self.fill()


def tile_of(n, size):
    return slice(n * size, (n + 1) * size)


def forward_kernel(
    large_hbm, gate_hbm, up_hbm, down_hbm, small_hbm, out_early_hbm, grad_early_hbm, a_hbm, b_hbm,
    large_ref, gate_ref, up_ref, down_ref, x_ref, grad_early_ref, product_ref, a_ref, b_ref, out_early_ref, small_ref,
    sems,
):
    size, width = BLOCK * CHUNKS, small_ref.shape[1]
    pairs, tiles = large_ref.shape[0] // (2 * size), gate_ref.shape[1] // FORWARD_TILE
    early = out_early_ref.shape[0]
    copies = Copies(sems)
    for i in range(pairs):
        copies.add(large_hbm.at[tile_of(i, 2 * size)], large_ref.at[tile_of(i, 2 * size)])
    for n in range(tiles):
        for source, target in ((gate_hbm, gate_ref), (up_hbm, up_ref)):
            copies.add(source.at[:, tile_of(n, FORWARD_TILE)], target.at[:, tile_of(n, FORWARD_TILE)])
    for c in range(CHUNKS):
        copies.add(down_hbm.at[:, tile_of(c, width)], down_ref.at[:, tile_of(c, width)])
    copies.fill()
    out = []

    perm = permutation(False, True)
    for i in range(pairs):
        copies.take()
        mixed_from_wire(large_ref, i * 2 * size, perm, i, early, x_ref, grad_early_ref)
    out.append(copies.start(grad_early_ref, grad_early_hbm))

    for n in range(tiles):
        copies.take(2)
        at = tile_of(n, FORWARD_TILE)
        hidden_a = dot(x_ref[...], gate_ref[:, at])
        hidden_b = dot(x_ref[...], up_ref[:, at])
        a_ref[:, at] = hidden_a
        b_ref[:, at] = hidden_b
        product_ref[:, at] = (hidden_a * jax.nn.sigmoid(hidden_a) * hidden_b).astype(bf16)
        out.append(copies.start(a_ref.at[:, at], a_hbm.at[:, at]))
        out.append(copies.start(b_ref.at[:, at], b_hbm.at[:, at]))

    for c in range(CHUNKS):
        copies.take()
        at = tile_of(c, width)
        rows = dot(product_ref[...], down_ref[:, at]).astype(bf16)
        out_early_ref[:, at] = rows[:early]
        x_ref[early:, at] = rows[early:]
        out.append(copies.start(out_early_ref.at[:, at], out_early_hbm.at[:, at]))

    perm = permutation(True, False)
    for i in range(small_ref.shape[0] // size):
        at = tile_of(i, size)
        small_ref[at, :] = to_wire(perm, x_ref[early + i * BLOCK : early + (i + 1) * BLOCK, :], width)
        out.append(copies.start(small_ref.at[at], small_hbm.at[at]))
    for copy in out:
        copy.wait()


def backward_kernel(
    small_hbm, grad_early_hbm, out_early_hbm, a_hbm, b_hbm, down_hbm, gate_hbm, up_hbm, large_hbm,
    small_ref, out_early_ref, a_ref, b_ref, down_ref, gate_ref, up_ref, x_ref, grad_a_ref, grad_b_ref, large_ref,
    sems,
):
    size, width = BLOCK * CHUNKS, large_ref.shape[1]
    pairs, tiles = large_ref.shape[0] // (2 * size), gate_ref.shape[1] // BACKWARD_TILE
    early = out_early_ref.shape[0]
    copies = Copies(sems)
    copies.add(small_hbm, small_ref)
    copies.add(grad_early_hbm, x_ref.at[:early])
    for n in range(tiles):
        at = tile_of(n, BACKWARD_TILE)
        copies.add(down_hbm.at[at], down_ref.at[at])
        copies.add(a_hbm.at[:, at], a_ref.at[:, at])
        copies.add(b_hbm.at[:, at], b_ref.at[:, at])
    for c in range(CHUNKS):
        at = tile_of(c, width)
        copies.add(gate_hbm.at[at], gate_ref.at[at])
        copies.add(up_hbm.at[at], up_ref.at[at])
    copies.add(out_early_hbm, out_early_ref)
    copies.fill()

    perm = permutation(False, False)
    copies.take()
    for i in range(small_ref.shape[0] // size):
        plain_from_wire(small_ref, i * size, perm, x_ref, early + i * BLOCK)
    copies.take()

    for n in range(tiles):
        copies.take(3)
        at = tile_of(n, BACKWARD_TILE)
        grad_act = dot_nt(x_ref[...], down_ref[at, :])
        hidden_a, hidden_b = a_ref[:, at], b_ref[:, at]
        sigmoid_a = jax.nn.sigmoid(hidden_a)
        slope = sigmoid_a * (1.0 + hidden_a * (1.0 - sigmoid_a))
        grad_a_ref[:, at] = (grad_act * hidden_b * slope).astype(bf16)
        grad_b_ref[:, at] = (grad_act * (hidden_a * sigmoid_a)).astype(bf16)

    for c in range(CHUNKS):
        copies.take(2)
        at = tile_of(c, width)
        rows = dot_nt(grad_a_ref[...], gate_ref[at, :]) + dot_nt(grad_b_ref[...], up_ref[at, :])
        x_ref[:, at] = rows.astype(bf16)

    copies.take()
    perm = permutation(True, True)
    out = []
    for i in range(pairs):
        ten, late = 2 * TEN_EARLY, 2 * TEN_LATE
        mixed_to_wire(
            large_ref,
            i * 2 * size,
            perm,
            x_ref[i * ten : (i + 1) * ten, :].astype(f32),
            x_ref[early + i * late : early + (i + 1) * late, :].astype(f32),
            out_early_ref[i * ten : (i + 1) * ten, :].astype(f32),
            width,
        )
        out.append(copies.start(large_ref.at[tile_of(i, 2 * size)], large_hbm.at[tile_of(i, 2 * size)]))
    for copy in out:
        copy.wait()


def expert_call(forward, args, slots, features, units):
    tiles = units // (FORWARD_TILE if forward else BACKWARD_TILE)
    width, size = features // CHUNKS, BLOCK * CHUNKS
    early = slots * EARLY // PER_CHIP
    large, small = slots * UNITS * CHUNKS // PER_CHIP, (slots - early) * CHUNKS
    pairs = large // (2 * size)

    def shape(*dims, dtype=bf16):
        return jax.ShapeDtypeStruct(dims, dtype)

    hidden = (slots, units)
    scratch = {
        "large": pltpu.VMEM((large, width), bf16),
        "small": pltpu.VMEM((small, width), bf16),
        "early": pltpu.VMEM((early, features), bf16),
        "x": pltpu.VMEM((slots, features), bf16),
        "wide": pltpu.VMEM(hidden, f32),
        "narrow": pltpu.VMEM(hidden, bf16),
        "up": pltpu.VMEM((features, units), bf16),
        "down": pltpu.VMEM((units, features), bf16),
    }
    if forward:
        kernel = forward_kernel
        out_shape = [
            shape(small, width), shape(early, features), shape(early, features),
            shape(*hidden, dtype=f32), shape(*hidden, dtype=f32),
        ]
        names = ("large", "up", "up", "down", "x", "early", "narrow", "wide", "wide", "early", "small")
        count = pairs + 4 * tiles + 1 + 2 * CHUNKS + small // size
    else:
        kernel = backward_kernel
        out_shape = shape(large, width)
        names = ("small", "early", "wide", "wide", "down", "up", "up", "x", "narrow", "narrow", "large")
        count = 3 + 3 * tiles + 2 * CHUNKS + pairs
    hbm = pl.BlockSpec(memory_space=pl.ANY)
    return pl.pallas_call(
        kernel,
        in_specs=[hbm] * len(args),
        out_specs=jax.tree.map(lambda _: hbm, out_shape),
        out_shape=out_shape,
        scratch_shapes=[scratch[name] for name in names] + [pltpu.SemaphoreType.DMA((count,))],
        compiler_params=pltpu.CompilerParams(vmem_limit_bytes=VMEM_LIMIT),
        cost_estimate=pl.CostEstimate(
            flops=6 * slots * units * features,
            bytes_accessed=6 * units * features + 6 * slots * features + 8 * slots * units,
            transcendentals=slots * units,
        ),
    )(*args)


def combine_kernel(
    small_ref, large_ref, pt_ref, hi_ref, lo_ref, out_own_ref, grad_own_ref, partner_ref,
    out_rows_ref, grad_rows_ref, mixed_ref, plain_ref,
):
    step = pl.program_id(0)
    size, width = BLOCK * CHUNKS, large_ref.shape[1]
    early = out_rows_ref.shape[0] * EARLY // PER_CHIP

    @pl.when(step == 0)
    def _():
        mixed_ref[...] = permutation(False, True)
        plain_ref[...] = permutation(False, False)

    pairs = large_ref.shape[0] // (2 * size)
    for i in range(pairs):
        mixed_from_wire(large_ref, i * 2 * size, mixed_ref[...], step * pairs + i, early, grad_rows_ref, out_rows_ref)
    for i in range(small_ref.shape[0] // size):
        start = early + step * (small_ref.shape[0] // CHUNKS) + i * BLOCK
        plain_from_wire(small_ref, i * size, plain_ref[...], out_rows_ref, start)

    @pl.when(step == pl.num_programs(0) - 1)
    def _():
        count = out_own_ref.shape[0]
        for c in range(CHUNKS):
            at = slice(c * width, (c + 1) * width)
            rows = out_rows_ref[:, at]
            total = dot(hi_ref[...], rows) + dot(lo_ref[...], rows)
            out_own_ref[:, at] = total[:count]
            partner_ref[0, :, at] = total[count:].astype(bf16)
            total = dot(pt_ref[...], grad_rows_ref[:, at])
            grad_own_ref[:, at] = total[:count]
            partner_ref[1, :, at] = total[count:].astype(bf16)


def combine(small, large, matrices, slots, rows, features):
    size, width = BLOCK * CHUNKS, features // CHUNKS
    steps = small.shape[0] // (GROUP * LATE * CHUNKS)
    matrix_spec = pl.BlockSpec((2 * rows, slots), lambda i: (0, 0))
    part_spec = pl.BlockSpec((rows, features), lambda i: (0, 0))
    return pl.pallas_call(
        combine_kernel,
        grid=(steps,),
        in_specs=[
            pl.BlockSpec((GROUP * LATE * CHUNKS, width), lambda i: (i, 0)),
            pl.BlockSpec((GROUP * UNITS * CHUNKS, width), lambda i: (i, 0)),
        ]
        + [matrix_spec] * 3,
        out_specs=[part_spec, part_spec, pl.BlockSpec((2, rows, features), lambda i: (0, 0, 0))],
        out_shape=[
            jax.ShapeDtypeStruct((rows, features), f32),
            jax.ShapeDtypeStruct((rows, features), f32),
            jax.ShapeDtypeStruct((2, rows, features), bf16),
        ],
        scratch_shapes=[
            pltpu.VMEM((slots, features), bf16),
            pltpu.VMEM((slots, features), bf16),
            pltpu.VMEM((size, size), bf16),
            pltpu.VMEM((size, size), bf16),
        ],
        compiler_params=pltpu.CompilerParams(vmem_limit_bytes=SMALL_LIMIT),
        cost_estimate=pl.CostEstimate(
            flops=4 * slots * (3 * rows + size) * features,
            bytes_accessed=4 * slots * features + 16 * rows * features,
            transcendentals=0,
        ),
    )(small, large, *matrices)


def local(tokens, grad_out, routes, gates, gate_weight, up_weight, down_weight):
    rows, features = tokens.shape
    units = gate_weight.shape[2]
    chips = lax.axis_size("dev")
    slots = chips * PER_CHIP
    role = lax.axis_index("role").astype(jnp.int32).reshape(1)
    swap = [(0, 1), (1, 0)]

    def other(array):
        return lax.ppermute(array, "role", swap)

    def exchange(wire):
        parts = wire.reshape(chips, wire.shape[0] // chips, wire.shape[1])
        parts = lax.all_to_all(parts, "dev", split_axis=0, concat_axis=0, tiled=True)
        return parts.reshape(wire.shape)

    route_lanes, gate_lanes = routes.T, gates.T
    route_other, gate_other = other(route_lanes), other(gate_lanes)
    p, slot_gate, *matrices = route(role, (route_lanes, route_other), (gate_lanes, gate_other), chips, slots)
    late_grad, _, _ = lax.optimization_barrier((grad_out, route_other, gate_other))
    large, small = pack(p, slot_gate, (tokens, other(tokens)), (grad_out, other(late_grad)), chips, slots)
    gate_local, up_local, down_local = gate_weight[0], up_weight[0], down_weight[0]

    large_in = exchange(large)
    small, _ = lax.optimization_barrier((small, large_in))
    small_in = exchange(small)
    small_out, out_early, grad_early, hidden_a, hidden_b = expert_call(
        True, (large_in, gate_local, up_local, down_local), slots, features, units
    )
    small_back = exchange(small_out)
    large_out = expert_call(
        False,
        (small_in, grad_early, out_early, hidden_a, hidden_b, down_local, gate_local, up_local),
        slots, features, units,
    )
    large_out, _ = lax.optimization_barrier((large_out, small_back))
    large_back = exchange(large_out)

    out_own, grad_own, partner = combine(small_back, large_back, matrices, slots, rows, features)
    received = other(partner).astype(f32)
    tokens_wide = tokens.astype(f32)
    layer_out = (tokens_wide + (out_own + received[0])).astype(bf16)
    grad_normed = grad_own + received[1]
    inv_rms = lax.rsqrt(jnp.mean(tokens_wide * tokens_wide, axis=1, keepdims=True) + epsilon)
    projected = jnp.mean(grad_normed * tokens_wide, axis=1, keepdims=True)
    grad_in = grad_out.astype(f32) + inv_rms * grad_normed - tokens_wide * inv_rms**3 * projected
    return (layer_out, grad_in.astype(bf16))


def solution(mesh):
    split = P(("role", "dev"), None)
    split_weight = P(("role", "dev"), None, None)
    in_specs = (split, split, split, split, split_weight, split_weight, split_weight)
    return jax.shard_map(local, mesh=mesh, in_specs=in_specs, out_specs=(split, split), check_vma=False)
```

```python
import functools
import math

import jax
import jax.numpy as jnp
from jax import lax
from jax.experimental import pallas as pl
from jax.experimental.pallas import tpu as pltpu
from jax.sharding import PartitionSpec as P

epsilon = 1e-06
bf16, f32 = jnp.bfloat16, jnp.float32
CHUNKS = 4
BLOCK = 64
EARLY = 6
PER_CHIP = 10
AHEAD = 5 * 1024 * 1024
FORWARD_TILE, BACKWARD_TILE = 256, 512
GROUP = 32
VMEM_LIMIT = 60 * 1024 * 1024
SMALL_LIMIT = 40 * 1024 * 1024


def dot(a, b):
    return jnp.dot(a, b, preferred_element_type=f32)


def dot_nt(a, b):
    return lax.dot_general(a, b, (((1,), (1,)), ((), ())), preferred_element_type=f32)


LATE = PER_CHIP - EARLY
UNITS = PER_CHIP + EARLY
SIDE = BLOCK // UNITS
TEN_EARLY, TEN_LATE = SIDE * EARLY, SIDE * LATE


def permutation(to_wire, mixed):
    size = BLOCK * CHUNKS
    wire = lax.broadcasted_iota(jnp.int32, (size, size), 0 if to_wire else 1)
    held = lax.broadcasted_iota(jnp.int32, (size, size), 1 if to_wire else 0)
    unit = lax.shift_right_logical(wire, 2)
    if mixed:
        chip, part = lax.shift_right_logical(unit, 4), unit & (UNITS - 1)
        six = TEN_EARLY + TEN_LATE + chip * EARLY + part - PER_CHIP
        late = TEN_EARLY + chip * LATE + part - EARLY
        unit = jnp.where(part < EARLY, chip * EARLY + part, jnp.where(part < PER_CHIP, late, six))
    return jnp.where((wire & (CHUNKS - 1)) * BLOCK + unit == held, 1.0, 0.0).astype(bf16)


def to_wire(perm, rows, width):
    stacked = jnp.concatenate([rows[:, c * width : (c + 1) * width] for c in range(CHUNKS)], axis=0)
    return dot(perm, stacked).astype(bf16)


def mixed_to_wire(out_ref, base, perm, ten_early, ten_late, six, width):
    size = BLOCK * CHUNKS
    for j in range(six.shape[0] // TEN_EARLY):
        rows = jnp.concatenate(
            [
                ten_early[j * TEN_EARLY : (j + 1) * TEN_EARLY],
                ten_late[j * TEN_LATE : (j + 1) * TEN_LATE],
                six[j * TEN_EARLY : (j + 1) * TEN_EARLY],
            ],
            axis=0,
        ).astype(bf16)
        out_ref[pl.ds(base + j * size, size), :] = to_wire(perm, rows, width)


def mixed_from_wire(wire_ref, base, perm, pair, early, ten_ref, six_ref):
    size, width = BLOCK * CHUNKS, wire_ref.shape[1]
    turned = [dot(perm, wire_ref[pl.ds(base + j * size, size), :]) for j in range(2)]
    edges = (0, TEN_EARLY, TEN_EARLY + TEN_LATE, BLOCK)
    places = (
        (ten_ref, pair * 2 * TEN_EARLY, 2 * TEN_EARLY),
        (ten_ref, early + pair * 2 * TEN_LATE, 2 * TEN_LATE),
        (six_ref, pair * 2 * TEN_EARLY, 2 * TEN_EARLY),
    )
    for n, (ref, start, count) in enumerate(places):
        at = pl.ds(pl.multiple_of(start, 16), count)
        for c in range(CHUNKS):
            rows = [t[c * BLOCK + edges[n] : c * BLOCK + edges[n + 1]] for t in turned]
            ref[at, c * width : (c + 1) * width] = jnp.concatenate(rows, axis=0).astype(bf16)


def plain_from_wire(wire_ref, base, perm, ref, start):
    size, width = BLOCK * CHUNKS, wire_ref.shape[1]
    turned = dot(perm, wire_ref[pl.ds(base, size), :]).astype(bf16)
    at = pl.ds(pl.multiple_of(start, 16), BLOCK)
    for c in range(CHUNKS):
        ref[at, c * width : (c + 1) * width] = turned[c * BLOCK : (c + 1) * BLOCK]


def slot_tables(chips, slots, rows):
    early = chips * EARLY
    cap = PER_CHIP // 2
    slot = lax.broadcasted_iota(jnp.int32, (slots, chips), 0)
    chip = lax.broadcasted_iota(jnp.int32, (slots, chips), 1)
    first = jnp.where(slot < early, chip * EARLY, early + chip * LATE)
    count = jnp.where(slot < early, EARLY, LATE)
    expand = jnp.where((slot >= first) & (slot < first + count), 1.0, 0.0)
    base = jnp.where(slot < early, first, first - EARLY).astype(f32)
    place = slot[:, :1].astype(f32) - jnp.sum(expand * base, axis=1, keepdims=True)
    partner = place >= cap
    rank = jnp.where(partner, place - cap, place) + 1.0
    lane = lax.broadcasted_iota(jnp.int32, (slots, 2 * rows), 1).astype(f32)
    side = jnp.where(partner, 1.0, 0.0)
    target = jnp.where(jnp.where(lane >= rows, 1.0, 0.0) == side, rank, -1.0)
    return expand.astype(bf16), target


def chosen_slots(role, sides, chips, slots):
    top, rows = sides[0][0].shape
    expand, target = slot_tables(chips, slots, rows)
    named = lax.broadcasted_iota(jnp.int32, (chips, rows), 0) + role * chips
    before = lax.broadcasted_iota(jnp.int32, (rows, rows), 0)
    after = lax.broadcasted_iota(jnp.int32, (rows, rows), 1)
    strict = jnp.where(before < after, 1.0, 0.0).astype(bf16)
    ranks, gates = [], []
    for route_ref, gate_ref in sides:
        uses = jnp.zeros((chips, rows), f32)
        gate = jnp.zeros((chips, rows), f32)
        for k in range(top):
            hit = named == route_ref[k : k + 1, :]
            uses = jnp.where(hit, 1.0, uses)
            gate = jnp.where(hit, gate_ref[k : k + 1, :], gate)
        ranks.append(uses * (dot(uses.astype(bf16), strict) + 1.0))
        gates.append(gate)
    rank = jnp.concatenate(ranks, axis=1).astype(bf16)
    gate = jnp.concatenate(gates, axis=1)
    chosen = dot(expand, rank) == target
    first = gate.astype(bf16)
    rest = gate - first.astype(f32)
    second = rest.astype(bf16)
    third = (rest - second.astype(f32)).astype(bf16)
    spread = dot(expand, first) + (dot(expand, second) + dot(expand, third))
    return jnp.where(chosen, 1.0, 0.0), jnp.where(chosen, spread, 0.0)


def route_kernel(
    chips, role_ref, route_ref, route_other_ref, gate_ref, gate_other_ref, p_ref, slot_gate_ref, pt_ref, hi_ref, lo_ref
):
    sides = ((route_ref, gate_ref), (route_other_ref, gate_other_ref))
    one_hot, spread = chosen_slots(role_ref[0], sides, chips, p_ref.shape[0])
    p_ref[...] = one_hot.astype(bf16)
    slot_gate_ref[...] = jnp.sum(spread, axis=1, keepdims=True)
    pt_ref[...] = jnp.transpose(one_hot).astype(bf16)
    turned = jnp.transpose(spread)
    hi = turned.astype(bf16)
    hi_ref[...] = hi
    lo_ref[...] = (turned - hi.astype(f32)).astype(bf16)


def route(role, routes, gates, chips, slots):
    rows = routes[0].shape[1]
    vmem = pl.BlockSpec(memory_space=pltpu.VMEM)
    turned_shape = jax.ShapeDtypeStruct((2 * rows, slots), bf16)
    return pl.pallas_call(
        functools.partial(route_kernel, chips),
        in_specs=[pl.BlockSpec(memory_space=pltpu.SMEM)] + [vmem] * 4,
        out_specs=[vmem] * 5,
        out_shape=[
            jax.ShapeDtypeStruct((slots, 2 * rows), bf16),
            jax.ShapeDtypeStruct((slots, 1), f32),
            turned_shape, turned_shape, turned_shape,
        ],
        compiler_params=pltpu.CompilerParams(vmem_limit_bytes=VMEM_LIMIT),
        cost_estimate=pl.CostEstimate(
            flops=8 * slots * rows * chips, bytes_accessed=12 * slots * rows, transcendentals=0
        ),
    )(role, *routes, *gates)


def pack_kernel(
    p_early_ref, p_late_ref, gate_early_ref, gate_late_ref, tokens_ref, tokens_other_ref, grad_ref, grad_other_ref,
    large_ref, small_ref, normed_ref, mixed_ref, plain_ref,
):
    tokens = tokens_ref.shape[0]
    width = large_ref.shape[1]

    @pl.when(pl.program_id(0) == 0)
    def _():
        mixed_ref[...] = permutation(True, True)
        plain_ref[...] = permutation(True, False)
        for i, ref in enumerate((tokens_ref, tokens_other_ref)):
            wide = ref[...].astype(f32)
            inv_rms = lax.rsqrt(jnp.mean(wide * wide, axis=1, keepdims=True) + epsilon)
            normed_ref[i * tokens : (i + 1) * tokens, :] = (wide * inv_rms).astype(bf16)

    early = p_early_ref.shape[0]
    p = jnp.concatenate([p_early_ref[...], p_late_ref[...]], axis=0)
    gate = jnp.concatenate([gate_early_ref[...], gate_late_ref[...]], axis=0)
    normed = dot(p, normed_ref[...])
    scaled = (dot(p[:, :tokens], grad_ref[...]) + dot(p[:, tokens:], grad_other_ref[...])) * gate
    mixed_to_wire(large_ref, 0, mixed_ref[...], normed[:early], normed[early:], scaled[:early], width)
    size = BLOCK * CHUNKS
    for i in range(small_ref.shape[0] // size):
        rows = scaled[early + i * BLOCK : early + (i + 1) * BLOCK].astype(bf16)
        small_ref[i * size : (i + 1) * size, :] = to_wire(plain_ref[...], rows, width)


def pack(p, slot_gate, tokens, grads, chips, slots):
    rows, features = tokens[0].shape
    width = features // CHUNKS
    late = chips * EARLY // (GROUP * LATE)
    size = BLOCK * CHUNKS
    rows_spec = pl.BlockSpec((rows, features), lambda i: (0, 0))
    large, small = GROUP * UNITS * CHUNKS, GROUP * LATE * CHUNKS
    steps = chips // GROUP
    return pl.pallas_call(
        pack_kernel,
        grid=(steps,),
        in_specs=[
            pl.BlockSpec((GROUP * EARLY, 2 * rows), lambda i: (i, 0)),
            pl.BlockSpec((GROUP * LATE, 2 * rows), lambda i: (late + i, 0)),
            pl.BlockSpec((GROUP * EARLY, 1), lambda i: (i, 0)),
            pl.BlockSpec((GROUP * LATE, 1), lambda i: (late + i, 0)),
        ]
        + [rows_spec] * 4,
        out_specs=[
            pl.BlockSpec((large, width), lambda i: (i, 0)),
            pl.BlockSpec((small, width), lambda i: (i, 0)),
        ],
        out_shape=[
            jax.ShapeDtypeStruct((steps * large, width), bf16),
            jax.ShapeDtypeStruct((steps * small, width), bf16),
        ],
        scratch_shapes=[
            pltpu.VMEM((2 * rows, features), bf16),
            pltpu.VMEM((size, size), bf16),
            pltpu.VMEM((size, size), bf16),
        ],
        compiler_params=pltpu.CompilerParams(vmem_limit_bytes=VMEM_LIMIT),
        cost_estimate=pl.CostEstimate(
            flops=4 * slots * (2 * rows + size) * features,
            bytes_accessed=4 * (2 * rows + slots) * features,
            transcendentals=0,
        ),
    )(p, p, slot_gate, slot_gate, *tokens, *grads)


class Copies:
    def __init__(self, sems):
        self.sems, self.made = sems, 0
        self.queue, self.flying, self.flying_bytes = [], [], 0

    def start(self, source, target):
        copy = pltpu.make_async_copy(source, target, self.sems.at[self.made])
        self.made += 1
        copy.start()
        return copy

    def add(self, source, target):
        self.queue.append((source, target, math.prod(target.shape) * target.dtype.itemsize))

    def fill(self):
        while self.queue and self.flying_bytes < AHEAD:
            source, target, size = self.queue.pop(0)
            self.flying.append((self.start(source, target), size))
            self.flying_bytes += size

    def take(self, count=1):
        for _ in range(count):
            self.fill()
            copy, size = self.flying.pop(0)
            copy.wait()
            self.flying_bytes -= size
        self.fill()


def tile_of(n, size):
    return slice(n * size, (n + 1) * size)


def forward_kernel(
    large_hbm, gate_hbm, up_hbm, down_hbm, small_hbm, out_early_hbm, grad_early_hbm, a_hbm, b_hbm,
    large_ref, gate_ref, up_ref, down_ref, x_ref, grad_early_ref, product_ref, a_ref, b_ref, out_early_ref, small_ref,
    sems,
):
    size, width = BLOCK * CHUNKS, small_ref.shape[1]
    pairs, tiles = large_ref.shape[0] // (2 * size), gate_ref.shape[1] // FORWARD_TILE
    early = out_early_ref.shape[0]
    copies = Copies(sems)
    for i in range(pairs):
        copies.add(large_hbm.at[tile_of(i, 2 * size)], large_ref.at[tile_of(i, 2 * size)])
    for n in range(tiles):
        for source, target in ((gate_hbm, gate_ref), (up_hbm, up_ref)):
            copies.add(source.at[:, tile_of(n, FORWARD_TILE)], target.at[:, tile_of(n, FORWARD_TILE)])
    for c in range(CHUNKS):
        copies.add(down_hbm.at[:, tile_of(c, width)], down_ref.at[:, tile_of(c, width)])
    copies.fill()
    out = []

    perm = permutation(False, True)
    for i in range(pairs):
        copies.take()
        mixed_from_wire(large_ref, i * 2 * size, perm, i, early, x_ref, grad_early_ref)
    out.append(copies.start(grad_early_ref, grad_early_hbm))

    for n in range(tiles):
        copies.take(2)
        at = tile_of(n, FORWARD_TILE)
        hidden_a = dot(x_ref[...], gate_ref[:, at])
        hidden_b = dot(x_ref[...], up_ref[:, at])
        a_ref[:, at] = hidden_a
        b_ref[:, at] = hidden_b
        product_ref[:, at] = (hidden_a * jax.nn.sigmoid(hidden_a) * hidden_b).astype(bf16)
        out.append(copies.start(a_ref.at[:, at], a_hbm.at[:, at]))
        out.append(copies.start(b_ref.at[:, at], b_hbm.at[:, at]))

    for c in range(CHUNKS):
        copies.take()
        at = tile_of(c, width)
        rows = dot(product_ref[...], down_ref[:, at]).astype(bf16)
        out_early_ref[:, at] = rows[:early]
        x_ref[early:, at] = rows[early:]
        out.append(copies.start(out_early_ref.at[:, at], out_early_hbm.at[:, at]))

    perm = permutation(True, False)
    for i in range(small_ref.shape[0] // size):
        at = tile_of(i, size)
        small_ref[at, :] = to_wire(perm, x_ref[early + i * BLOCK : early + (i + 1) * BLOCK, :], width)
        out.append(copies.start(small_ref.at[at], small_hbm.at[at]))
    for copy in out:
        copy.wait()


def backward_kernel(
    small_hbm, grad_early_hbm, out_early_hbm, a_hbm, b_hbm, down_hbm, gate_hbm, up_hbm, large_hbm,
    small_ref, out_early_ref, a_ref, b_ref, down_ref, gate_ref, up_ref, x_ref, grad_a_ref, grad_b_ref, large_ref,
    sems,
):
    size, width = BLOCK * CHUNKS, large_ref.shape[1]
    pairs, tiles = large_ref.shape[0] // (2 * size), gate_ref.shape[1] // BACKWARD_TILE
    early = out_early_ref.shape[0]
    copies = Copies(sems)
    copies.add(small_hbm, small_ref)
    copies.add(grad_early_hbm, x_ref.at[:early])
    for n in range(tiles):
        at = tile_of(n, BACKWARD_TILE)
        copies.add(down_hbm.at[at], down_ref.at[at])
        copies.add(a_hbm.at[:, at], a_ref.at[:, at])
        copies.add(b_hbm.at[:, at], b_ref.at[:, at])
    for c in range(CHUNKS):
        at = tile_of(c, width)
        copies.add(gate_hbm.at[at], gate_ref.at[at])
        copies.add(up_hbm.at[at], up_ref.at[at])
    copies.add(out_early_hbm, out_early_ref)
    copies.fill()

    perm = permutation(False, False)
    copies.take()
    for i in range(small_ref.shape[0] // size):
        plain_from_wire(small_ref, i * size, perm, x_ref, early + i * BLOCK)
    copies.take()

    for n in range(tiles):
        copies.take(3)
        at = tile_of(n, BACKWARD_TILE)
        grad_act = dot_nt(x_ref[...], down_ref[at, :])
        hidden_a, hidden_b = a_ref[:, at], b_ref[:, at]
        sigmoid_a = jax.nn.sigmoid(hidden_a)
        slope = sigmoid_a * (1.0 + hidden_a * (1.0 - sigmoid_a))
        grad_a_ref[:, at] = (grad_act * hidden_b * slope).astype(bf16)
        grad_b_ref[:, at] = (grad_act * (hidden_a * sigmoid_a)).astype(bf16)

    for c in range(CHUNKS):
        copies.take(2)
        at = tile_of(c, width)
        rows = dot_nt(grad_a_ref[...], gate_ref[at, :]) + dot_nt(grad_b_ref[...], up_ref[at, :])
        x_ref[:, at] = rows.astype(bf16)

    copies.take()
    perm = permutation(True, True)
    out = []
    for i in range(pairs):
        ten, late = 2 * TEN_EARLY, 2 * TEN_LATE
        mixed_to_wire(
            large_ref,
            i * 2 * size,
            perm,
            x_ref[i * ten : (i + 1) * ten, :].astype(f32),
            x_ref[early + i * late : early + (i + 1) * late, :].astype(f32),
            out_early_ref[i * ten : (i + 1) * ten, :].astype(f32),
            width,
        )
        out.append(copies.start(large_ref.at[tile_of(i, 2 * size)], large_hbm.at[tile_of(i, 2 * size)]))
    for copy in out:
        copy.wait()


def expert_call(forward, args, slots, features, units):
    tiles = units // (FORWARD_TILE if forward else BACKWARD_TILE)
    width, size = features // CHUNKS, BLOCK * CHUNKS
    early = slots * EARLY // PER_CHIP
    large, small = slots * UNITS * CHUNKS // PER_CHIP, (slots - early) * CHUNKS
    pairs = large // (2 * size)

    def shape(*dims, dtype=bf16):
        return jax.ShapeDtypeStruct(dims, dtype)

    hidden = (slots, units)
    scratch = {
        "large": pltpu.VMEM((large, width), bf16),
        "small": pltpu.VMEM((small, width), bf16),
        "early": pltpu.VMEM((early, features), bf16),
        "x": pltpu.VMEM((slots, features), bf16),
        "wide": pltpu.VMEM(hidden, f32),
        "narrow": pltpu.VMEM(hidden, bf16),
        "up": pltpu.VMEM((features, units), bf16),
        "down": pltpu.VMEM((units, features), bf16),
    }
    if forward:
        kernel = forward_kernel
        out_shape = [
            shape(small, width), shape(early, features), shape(early, features),
            shape(*hidden, dtype=f32), shape(*hidden, dtype=f32),
        ]
        names = ("large", "up", "up", "down", "x", "early", "narrow", "wide", "wide", "early", "small")
        count = pairs + 4 * tiles + 1 + 2 * CHUNKS + small // size
    else:
        kernel = backward_kernel
        out_shape = shape(large, width)
        names = ("small", "early", "wide", "wide", "down", "up", "up", "x", "narrow", "narrow", "large")
        count = 3 + 3 * tiles + 2 * CHUNKS + pairs
    hbm = pl.BlockSpec(memory_space=pl.ANY)
    return pl.pallas_call(
        kernel,
        in_specs=[hbm] * len(args),
        out_specs=jax.tree.map(lambda _: hbm, out_shape),
        out_shape=out_shape,
        scratch_shapes=[scratch[name] for name in names] + [pltpu.SemaphoreType.DMA((count,))],
        compiler_params=pltpu.CompilerParams(vmem_limit_bytes=VMEM_LIMIT),
        cost_estimate=pl.CostEstimate(
            flops=6 * slots * units * features,
            bytes_accessed=6 * units * features + 6 * slots * features + 8 * slots * units,
            transcendentals=slots * units,
        ),
    )(*args)


def combine_kernel(
    small_ref, large_ref, pt_ref, hi_ref, lo_ref, out_own_ref, grad_own_ref, partner_ref,
    out_rows_ref, grad_rows_ref, mixed_ref, plain_ref,
):
    step = pl.program_id(0)
    size, width = BLOCK * CHUNKS, large_ref.shape[1]
    early = out_rows_ref.shape[0] * EARLY // PER_CHIP

    @pl.when(step == 0)
    def _():
        mixed_ref[...] = permutation(False, True)
        plain_ref[...] = permutation(False, False)

    pairs = large_ref.shape[0] // (2 * size)
    for i in range(pairs):
        mixed_from_wire(large_ref, i * 2 * size, mixed_ref[...], step * pairs + i, early, grad_rows_ref, out_rows_ref)
    for i in range(small_ref.shape[0] // size):
        start = early + step * (small_ref.shape[0] // CHUNKS) + i * BLOCK
        plain_from_wire(small_ref, i * size, plain_ref[...], out_rows_ref, start)

    @pl.when(step == pl.num_programs(0) - 1)
    def _():
        count = out_own_ref.shape[0]
        for c in range(CHUNKS):
            at = slice(c * width, (c + 1) * width)
            rows = out_rows_ref[:, at]
            total = dot(hi_ref[...], rows) + dot(lo_ref[...], rows)
            out_own_ref[:, at] = total[:count]
            partner_ref[0, :, at] = total[count:].astype(bf16)
            total = dot(pt_ref[...], grad_rows_ref[:, at])
            grad_own_ref[:, at] = total[:count]
            partner_ref[1, :, at] = total[count:].astype(bf16)


def combine(small, large, matrices, slots, rows, features):
    size, width = BLOCK * CHUNKS, features // CHUNKS
    steps = small.shape[0] // (GROUP * LATE * CHUNKS)
    matrix_spec = pl.BlockSpec((2 * rows, slots), lambda i: (0, 0))
    part_spec = pl.BlockSpec((rows, features), lambda i: (0, 0))
    return pl.pallas_call(
        combine_kernel,
        grid=(steps,),
        in_specs=[
            pl.BlockSpec((GROUP * LATE * CHUNKS, width), lambda i: (i, 0)),
            pl.BlockSpec((GROUP * UNITS * CHUNKS, width), lambda i: (i, 0)),
        ]
        + [matrix_spec] * 3,
        out_specs=[part_spec, part_spec, pl.BlockSpec((2, rows, features), lambda i: (0, 0, 0))],
        out_shape=[
            jax.ShapeDtypeStruct((rows, features), f32),
            jax.ShapeDtypeStruct((rows, features), f32),
            jax.ShapeDtypeStruct((2, rows, features), bf16),
        ],
        scratch_shapes=[
            pltpu.VMEM((slots, features), bf16),
            pltpu.VMEM((slots, features), bf16),
            pltpu.VMEM((size, size), bf16),
            pltpu.VMEM((size, size), bf16),
        ],
        compiler_params=pltpu.CompilerParams(vmem_limit_bytes=SMALL_LIMIT),
        cost_estimate=pl.CostEstimate(
            flops=4 * slots * (3 * rows + size) * features,
            bytes_accessed=4 * slots * features + 16 * rows * features,
            transcendentals=0,
        ),
    )(small, large, *matrices)


def local(tokens, grad_out, routes, gates, gate_weight, up_weight, down_weight):
    rows, features = tokens.shape
    units = gate_weight.shape[2]
    chips = lax.axis_size("dev")
    slots = chips * PER_CHIP
    role = lax.axis_index("role").astype(jnp.int32).reshape(1)
    swap = [(0, 1), (1, 0)]

    def other(array):
        return lax.ppermute(array, "role", swap)

    def exchange(wire):
        parts = wire.reshape(chips, wire.shape[0] // chips, wire.shape[1])
        parts = lax.all_to_all(parts, "dev", split_axis=0, concat_axis=0, tiled=True)
        return parts.reshape(wire.shape)

    route_lanes, gate_lanes = routes.T, gates.T
    route_other, gate_other = other(route_lanes), other(gate_lanes)
    p, slot_gate, *matrices = route(role, (route_lanes, route_other), (gate_lanes, gate_other), chips, slots)
    late_grad, _, _ = lax.optimization_barrier((grad_out, route_other, gate_other))
    large, small = pack(p, slot_gate, (tokens, other(tokens)), (grad_out, other(late_grad)), chips, slots)
    gate_local, up_local, down_local = gate_weight[0], up_weight[0], down_weight[0]

    large_in = exchange(large)
    small, _ = lax.optimization_barrier((small, large_in))
    small_in = exchange(small)
    small_out, out_early, grad_early, hidden_a, hidden_b = expert_call(
        True, (large_in, gate_local, up_local, down_local), slots, features, units
    )
    small_back = exchange(small_out)
    large_out = expert_call(
        False,
        (small_in, grad_early, out_early, hidden_a, hidden_b, down_local, gate_local, up_local),
        slots, features, units,
    )
    large_out, _ = lax.optimization_barrier((large_out, small_back))
    large_back = exchange(large_out)

    out_own, grad_own, partner = combine(small_back, large_back, matrices, slots, rows, features)
    received = other(partner).astype(f32)
    tokens_wide = tokens.astype(f32)
    layer_out = (tokens_wide + (out_own + received[0])).astype(bf16)
    grad_normed = grad_own + received[1]
    inv_rms = lax.rsqrt(jnp.mean(tokens_wide * tokens_wide, axis=1, keepdims=True) + epsilon)
    projected = jnp.mean(grad_normed * tokens_wide, axis=1, keepdims=True)
    grad_in = grad_out.astype(f32) + inv_rms * grad_normed - tokens_wide * inv_rms**3 * projected
    return (layer_out, grad_in.astype(bf16))


def solution(mesh):
    split = P(("role", "dev"), None)
    split_weight = P(("role", "dev"), None, None)
    in_specs = (split, split, split, split, split_weight, split_weight, split_weight)
    return jax.shard_map(local, mesh=mesh, in_specs=in_specs, out_specs=(split, split), check_vma=False)
```

```python
import functools
import math

import jax
import jax.numpy as jnp
from jax import lax
from jax.experimental import pallas as pl
from jax.experimental.pallas import tpu as pltpu
from jax.sharding import PartitionSpec as P

epsilon = 1e-06
bf16, f32 = jnp.bfloat16, jnp.float32
CHUNKS = 4
BLOCK = 64
EARLY = 6
PER_CHIP = 10
AHEAD = 5 * 1024 * 1024
FORWARD_TILE, BACKWARD_TILE = 256, 512
GROUP = 32
VMEM_LIMIT = 60 * 1024 * 1024
SMALL_LIMIT = 40 * 1024 * 1024


def dot(a, b):
    return jnp.dot(a, b, preferred_element_type=f32)


def dot_nt(a, b):
    return lax.dot_general(a, b, (((1,), (1,)), ((), ())), preferred_element_type=f32)


LATE = PER_CHIP - EARLY
UNITS = PER_CHIP + EARLY
SIDE = BLOCK // UNITS
TEN_EARLY, TEN_LATE = SIDE * EARLY, SIDE * LATE


def permutation(to_wire, mixed):
    size = BLOCK * CHUNKS
    wire = lax.broadcasted_iota(jnp.int32, (size, size), 0 if to_wire else 1)
    held = lax.broadcasted_iota(jnp.int32, (size, size), 1 if to_wire else 0)
    unit = lax.shift_right_logical(wire, 2)
    if mixed:
        chip, part = lax.shift_right_logical(unit, 4), unit & (UNITS - 1)
        six = TEN_EARLY + TEN_LATE + chip * EARLY + part - PER_CHIP
        late = TEN_EARLY + chip * LATE + part - EARLY
        unit = jnp.where(part < EARLY, chip * EARLY + part, jnp.where(part < PER_CHIP, late, six))
    return jnp.where((wire & (CHUNKS - 1)) * BLOCK + unit == held, 1.0, 0.0).astype(bf16)


def to_wire(perm, rows, width):
    stacked = jnp.concatenate([rows[:, c * width : (c + 1) * width] for c in range(CHUNKS)], axis=0)
    return dot(perm, stacked).astype(bf16)


def mixed_to_wire(out_ref, base, perm, ten_early, ten_late, six, width):
    size = BLOCK * CHUNKS
    for j in range(six.shape[0] // TEN_EARLY):
        rows = jnp.concatenate(
            [
                ten_early[j * TEN_EARLY : (j + 1) * TEN_EARLY],
                ten_late[j * TEN_LATE : (j + 1) * TEN_LATE],
                six[j * TEN_EARLY : (j + 1) * TEN_EARLY],
            ],
            axis=0,
        ).astype(bf16)
        out_ref[pl.ds(base + j * size, size), :] = to_wire(perm, rows, width)


def mixed_from_wire(wire_ref, base, perm, pair, early, ten_ref, six_ref):
    size, width = BLOCK * CHUNKS, wire_ref.shape[1]
    turned = [dot(perm, wire_ref[pl.ds(base + j * size, size), :]) for j in range(2)]
    edges = (0, TEN_EARLY, TEN_EARLY + TEN_LATE, BLOCK)
    places = (
        (ten_ref, pair * 2 * TEN_EARLY, 2 * TEN_EARLY),
        (ten_ref, early + pair * 2 * TEN_LATE, 2 * TEN_LATE),
        (six_ref, pair * 2 * TEN_EARLY, 2 * TEN_EARLY),
    )
    for n, (ref, start, count) in enumerate(places):
        at = pl.ds(pl.multiple_of(start, 16), count)
        for c in range(CHUNKS):
            rows = [t[c * BLOCK + edges[n] : c * BLOCK + edges[n + 1]] for t in turned]
            ref[at, c * width : (c + 1) * width] = jnp.concatenate(rows, axis=0).astype(bf16)


def plain_from_wire(wire_ref, base, perm, ref, start):
    size, width = BLOCK * CHUNKS, wire_ref.shape[1]
    turned = dot(perm, wire_ref[pl.ds(base, size), :]).astype(bf16)
    at = pl.ds(pl.multiple_of(start, 16), BLOCK)
    for c in range(CHUNKS):
        ref[at, c * width : (c + 1) * width] = turned[c * BLOCK : (c + 1) * BLOCK]


def slot_tables(chips, slots, rows):
    early = chips * EARLY
    cap = PER_CHIP // 2
    slot = lax.broadcasted_iota(jnp.int32, (slots, chips), 0)
    chip = lax.broadcasted_iota(jnp.int32, (slots, chips), 1)
    first = jnp.where(slot < early, chip * EARLY, early + chip * LATE)
    count = jnp.where(slot < early, EARLY, LATE)
    expand = jnp.where((slot >= first) & (slot < first + count), 1.0, 0.0)
    base = jnp.where(slot < early, first, first - EARLY).astype(f32)
    place = slot[:, :1].astype(f32) - jnp.sum(expand * base, axis=1, keepdims=True)
    partner = place >= cap
    rank = jnp.where(partner, place - cap, place) + 1.0
    lane = lax.broadcasted_iota(jnp.int32, (slots, 2 * rows), 1).astype(f32)
    side = jnp.where(partner, 1.0, 0.0)
    target = jnp.where(jnp.where(lane >= rows, 1.0, 0.0) == side, rank, -1.0)
    return expand.astype(bf16), target


def chosen_slots(role, sides, chips, slots):
    top, rows = sides[0][0].shape
    expand, target = slot_tables(chips, slots, rows)
    named = lax.broadcasted_iota(jnp.int32, (chips, rows), 0) + role * chips
    before = lax.broadcasted_iota(jnp.int32, (rows, rows), 0)
    after = lax.broadcasted_iota(jnp.int32, (rows, rows), 1)
    strict = jnp.where(before < after, 1.0, 0.0).astype(bf16)
    ranks, gates = [], []
    for route_ref, gate_ref in sides:
        uses = jnp.zeros((chips, rows), f32)
        gate = jnp.zeros((chips, rows), f32)
        for k in range(top):
            hit = named == route_ref[k : k + 1, :]
            uses = jnp.where(hit, 1.0, uses)
            gate = jnp.where(hit, gate_ref[k : k + 1, :], gate)
        ranks.append(uses * (dot(uses.astype(bf16), strict) + 1.0))
        gates.append(gate)
    rank = jnp.concatenate(ranks, axis=1).astype(bf16)
    gate = jnp.concatenate(gates, axis=1)
    chosen = dot(expand, rank) == target
    first = gate.astype(bf16)
    rest = gate - first.astype(f32)
    second = rest.astype(bf16)
    third = (rest - second.astype(f32)).astype(bf16)
    spread = dot(expand, first) + (dot(expand, second) + dot(expand, third))
    return jnp.where(chosen, 1.0, 0.0), jnp.where(chosen, spread, 0.0)


def route_kernel(
    chips, role_ref, route_ref, route_other_ref, gate_ref, gate_other_ref, p_ref, slot_gate_ref, pt_ref, hi_ref, lo_ref
):
    sides = ((route_ref, gate_ref), (route_other_ref, gate_other_ref))
    one_hot, spread = chosen_slots(role_ref[0], sides, chips, p_ref.shape[0])
    p_ref[...] = one_hot.astype(bf16)
    slot_gate_ref[...] = jnp.sum(spread, axis=1, keepdims=True)
    pt_ref[...] = jnp.transpose(one_hot).astype(bf16)
    turned = jnp.transpose(spread)
    hi = turned.astype(bf16)
    hi_ref[...] = hi
    lo_ref[...] = (turned - hi.astype(f32)).astype(bf16)


def route(role, routes, gates, chips, slots):
    rows = routes[0].shape[1]
    vmem = pl.BlockSpec(memory_space=pltpu.VMEM)
    turned_shape = jax.ShapeDtypeStruct((2 * rows, slots), bf16)
    return pl.pallas_call(
        functools.partial(route_kernel, chips),
        in_specs=[pl.BlockSpec(memory_space=pltpu.SMEM)] + [vmem] * 4,
        out_specs=[vmem] * 5,
        out_shape=[
            jax.ShapeDtypeStruct((slots, 2 * rows), bf16),
            jax.ShapeDtypeStruct((slots, 1), f32),
            turned_shape, turned_shape, turned_shape,
        ],
        compiler_params=pltpu.CompilerParams(vmem_limit_bytes=VMEM_LIMIT),
        cost_estimate=pl.CostEstimate(
            flops=8 * slots * rows * chips, bytes_accessed=12 * slots * rows, transcendentals=0
        ),
    )(role, *routes, *gates)


def pack_kernel(
    p_early_ref, p_late_ref, gate_early_ref, gate_late_ref, tokens_ref, tokens_other_ref, grad_ref, grad_other_ref,
    large_ref, small_ref, normed_ref, mixed_ref, plain_ref,
):
    tokens = tokens_ref.shape[0]
    width = large_ref.shape[1]

    @pl.when(pl.program_id(0) == 0)
    def _():
        mixed_ref[...] = permutation(True, True)
        plain_ref[...] = permutation(True, False)
        for i, ref in enumerate((tokens_ref, tokens_other_ref)):
            wide = ref[...].astype(f32)
            inv_rms = lax.rsqrt(jnp.mean(wide * wide, axis=1, keepdims=True) + epsilon)
            normed_ref[i * tokens : (i + 1) * tokens, :] = (wide * inv_rms).astype(bf16)

    early = p_early_ref.shape[0]
    p = jnp.concatenate([p_early_ref[...], p_late_ref[...]], axis=0)
    gate = jnp.concatenate([gate_early_ref[...], gate_late_ref[...]], axis=0)
    normed = dot(p, normed_ref[...])
    scaled = (dot(p[:, :tokens], grad_ref[...]) + dot(p[:, tokens:], grad_other_ref[...])) * gate
    mixed_to_wire(large_ref, 0, mixed_ref[...], normed[:early], normed[early:], scaled[:early], width)
    size = BLOCK * CHUNKS
    for i in range(small_ref.shape[0] // size):
        rows = scaled[early + i * BLOCK : early + (i + 1) * BLOCK].astype(bf16)
        small_ref[i * size : (i + 1) * size, :] = to_wire(plain_ref[...], rows, width)


def pack(p, slot_gate, tokens, grads, chips, slots):
    rows, features = tokens[0].shape
    width = features // CHUNKS
    late = chips * EARLY // (GROUP * LATE)
    size = BLOCK * CHUNKS
    rows_spec = pl.BlockSpec((rows, features), lambda i: (0, 0))
    large, small = GROUP * UNITS * CHUNKS, GROUP * LATE * CHUNKS
    steps = chips // GROUP
    return pl.pallas_call(
        pack_kernel,
        grid=(steps,),
        in_specs=[
            pl.BlockSpec((GROUP * EARLY, 2 * rows), lambda i: (i, 0)),
            pl.BlockSpec((GROUP * LATE, 2 * rows), lambda i: (late + i, 0)),
            pl.BlockSpec((GROUP * EARLY, 1), lambda i: (i, 0)),
            pl.BlockSpec((GROUP * LATE, 1), lambda i: (late + i, 0)),
        ]
        + [rows_spec] * 4,
        out_specs=[
            pl.BlockSpec((large, width), lambda i: (i, 0)),
            pl.BlockSpec((small, width), lambda i: (i, 0)),
        ],
        out_shape=[
            jax.ShapeDtypeStruct((steps * large, width), bf16),
            jax.ShapeDtypeStruct((steps * small, width), bf16),
        ],
        scratch_shapes=[
            pltpu.VMEM((2 * rows, features), bf16),
            pltpu.VMEM((size, size), bf16),
            pltpu.VMEM((size, size), bf16),
        ],
        compiler_params=pltpu.CompilerParams(vmem_limit_bytes=VMEM_LIMIT),
        cost_estimate=pl.CostEstimate(
            flops=4 * slots * (2 * rows + size) * features,
            bytes_accessed=4 * (2 * rows + slots) * features,
            transcendentals=0,
        ),
    )(p, p, slot_gate, slot_gate, *tokens, *grads)


class Copies:
    def __init__(self, sems):
        self.sems, self.made = sems, 0
        self.queue, self.flying, self.flying_bytes = [], [], 0

    def start(self, source, target):
        copy = pltpu.make_async_copy(source, target, self.sems.at[self.made])
        self.made += 1
        copy.start()
        return copy

    def add(self, source, target):
        self.queue.append((source, target, math.prod(target.shape) * target.dtype.itemsize))

    def fill(self):
        while self.queue and self.flying_bytes < AHEAD:
            source, target, size = self.queue.pop(0)
            self.flying.append((self.start(source, target), size))
            self.flying_bytes += size

    def take(self, count=1):
        for _ in range(count):
            self.fill()
            copy, size = self.flying.pop(0)
            copy.wait()
            self.flying_bytes -= size
        self.fill()


def tile_of(n, size):
    return slice(n * size, (n + 1) * size)


def forward_kernel(
    large_hbm, gate_hbm, up_hbm, down_hbm, small_hbm, out_early_hbm, grad_early_hbm, a_hbm, b_hbm,
    large_ref, gate_ref, up_ref, down_ref, x_ref, grad_early_ref, product_ref, a_ref, b_ref, out_early_ref, small_ref,
    sems,
):
    size, width = BLOCK * CHUNKS, small_ref.shape[1]
    pairs, tiles = large_ref.shape[0] // (2 * size), gate_ref.shape[1] // FORWARD_TILE
    early = out_early_ref.shape[0]
    copies = Copies(sems)
    for i in range(pairs):
        copies.add(large_hbm.at[tile_of(i, 2 * size)], large_ref.at[tile_of(i, 2 * size)])
    for n in range(tiles):
        for source, target in ((gate_hbm, gate_ref), (up_hbm, up_ref)):
            copies.add(source.at[:, tile_of(n, FORWARD_TILE)], target.at[:, tile_of(n, FORWARD_TILE)])
    for c in range(CHUNKS):
        copies.add(down_hbm.at[:, tile_of(c, width)], down_ref.at[:, tile_of(c, width)])
    copies.fill()
    out = []

    perm = permutation(False, True)
    for i in range(pairs):
        copies.take()
        mixed_from_wire(large_ref, i * 2 * size, perm, i, early, x_ref, grad_early_ref)
    out.append(copies.start(grad_early_ref, grad_early_hbm))

    for n in range(tiles):
        copies.take(2)
        at = tile_of(n, FORWARD_TILE)
        hidden_a = dot(x_ref[...], gate_ref[:, at])
        hidden_b = dot(x_ref[...], up_ref[:, at])
        a_ref[:, at] = hidden_a
        b_ref[:, at] = hidden_b
        product_ref[:, at] = (hidden_a * jax.nn.sigmoid(hidden_a) * hidden_b).astype(bf16)
        out.append(copies.start(a_ref.at[:, at], a_hbm.at[:, at]))
        out.append(copies.start(b_ref.at[:, at], b_hbm.at[:, at]))

    for c in range(CHUNKS):
        copies.take()
        at = tile_of(c, width)
        rows = dot(product_ref[...], down_ref[:, at]).astype(bf16)
        out_early_ref[:, at] = rows[:early]
        x_ref[early:, at] = rows[early:]
        out.append(copies.start(out_early_ref.at[:, at], out_early_hbm.at[:, at]))

    perm = permutation(True, False)
    for i in range(small_ref.shape[0] // size):
        at = tile_of(i, size)
        small_ref[at, :] = to_wire(perm, x_ref[early + i * BLOCK : early + (i + 1) * BLOCK, :], width)
        out.append(copies.start(small_ref.at[at], small_hbm.at[at]))
    for copy in out:
        copy.wait()


def backward_kernel(
    small_hbm, grad_early_hbm, out_early_hbm, a_hbm, b_hbm, down_hbm, gate_hbm, up_hbm, large_hbm,
    small_ref, out_early_ref, a_ref, b_ref, down_ref, gate_ref, up_ref, x_ref, grad_a_ref, grad_b_ref, large_ref,
    sems,
):
    size, width = BLOCK * CHUNKS, large_ref.shape[1]
    pairs, tiles = large_ref.shape[0] // (2 * size), gate_ref.shape[1] // BACKWARD_TILE
    early = out_early_ref.shape[0]
    copies = Copies(sems)
    copies.add(small_hbm, small_ref)
    copies.add(grad_early_hbm, x_ref.at[:early])
    for n in range(tiles):
        at = tile_of(n, BACKWARD_TILE)
        copies.add(down_hbm.at[at], down_ref.at[at])
        copies.add(a_hbm.at[:, at], a_ref.at[:, at])
        copies.add(b_hbm.at[:, at], b_ref.at[:, at])
    for c in range(CHUNKS):
        at = tile_of(c, width)
        copies.add(gate_hbm.at[at], gate_ref.at[at])
        copies.add(up_hbm.at[at], up_ref.at[at])
    copies.add(out_early_hbm, out_early_ref)
    copies.fill()

    perm = permutation(False, False)
    copies.take()
    for i in range(small_ref.shape[0] // size):
        plain_from_wire(small_ref, i * size, perm, x_ref, early + i * BLOCK)
    copies.take()

    for n in range(tiles):
        copies.take(3)
        at = tile_of(n, BACKWARD_TILE)
        grad_act = dot_nt(x_ref[...], down_ref[at, :])
        hidden_a, hidden_b = a_ref[:, at], b_ref[:, at]
        sigmoid_a = jax.nn.sigmoid(hidden_a)
        slope = sigmoid_a * (1.0 + hidden_a * (1.0 - sigmoid_a))
        grad_a_ref[:, at] = (grad_act * hidden_b * slope).astype(bf16)
        grad_b_ref[:, at] = (grad_act * (hidden_a * sigmoid_a)).astype(bf16)

    for c in range(CHUNKS):
        copies.take(2)
        at = tile_of(c, width)
        rows = dot_nt(grad_a_ref[...], gate_ref[at, :]) + dot_nt(grad_b_ref[...], up_ref[at, :])
        x_ref[:, at] = rows.astype(bf16)

    copies.take()
    perm = permutation(True, True)
    out = []
    for i in range(pairs):
        ten, late = 2 * TEN_EARLY, 2 * TEN_LATE
        mixed_to_wire(
            large_ref,
            i * 2 * size,
            perm,
            x_ref[i * ten : (i + 1) * ten, :].astype(f32),
            x_ref[early + i * late : early + (i + 1) * late, :].astype(f32),
            out_early_ref[i * ten : (i + 1) * ten, :].astype(f32),
            width,
        )
        out.append(copies.start(large_ref.at[tile_of(i, 2 * size)], large_hbm.at[tile_of(i, 2 * size)]))
    for copy in out:
        copy.wait()


def expert_call(forward, args, slots, features, units):
    tiles = units // (FORWARD_TILE if forward else BACKWARD_TILE)
    width, size = features // CHUNKS, BLOCK * CHUNKS
    early = slots * EARLY // PER_CHIP
    large, small = slots * UNITS * CHUNKS // PER_CHIP, (slots - early) * CHUNKS
    pairs = large // (2 * size)

    def shape(*dims, dtype=bf16):
        return jax.ShapeDtypeStruct(dims, dtype)

    hidden = (slots, units)
    scratch = {
        "large": pltpu.VMEM((large, width), bf16),
        "small": pltpu.VMEM((small, width), bf16),
        "early": pltpu.VMEM((early, features), bf16),
        "x": pltpu.VMEM((slots, features), bf16),
        "wide": pltpu.VMEM(hidden, f32),
        "narrow": pltpu.VMEM(hidden, bf16),
        "up": pltpu.VMEM((features, units), bf16),
        "down": pltpu.VMEM((units, features), bf16),
    }
    if forward:
        kernel = forward_kernel
        out_shape = [
            shape(small, width), shape(early, features), shape(early, features),
            shape(*hidden, dtype=f32), shape(*hidden, dtype=f32),
        ]
        names = ("large", "up", "up", "down", "x", "early", "narrow", "wide", "wide", "early", "small")
        count = pairs + 4 * tiles + 1 + 2 * CHUNKS + small // size
    else:
        kernel = backward_kernel
        out_shape = shape(large, width)
        names = ("small", "early", "wide", "wide", "down", "up", "up", "x", "narrow", "narrow", "large")
        count = 3 + 3 * tiles + 2 * CHUNKS + pairs
    hbm = pl.BlockSpec(memory_space=pl.ANY)
    return pl.pallas_call(
        kernel,
        in_specs=[hbm] * len(args),
        out_specs=jax.tree.map(lambda _: hbm, out_shape),
        out_shape=out_shape,
        scratch_shapes=[scratch[name] for name in names] + [pltpu.SemaphoreType.DMA((count,))],
        compiler_params=pltpu.CompilerParams(vmem_limit_bytes=VMEM_LIMIT),
        cost_estimate=pl.CostEstimate(
            flops=6 * slots * units * features,
            bytes_accessed=6 * units * features + 6 * slots * features + 8 * slots * units,
            transcendentals=slots * units,
        ),
    )(*args)


def combine_kernel(
    small_ref, large_ref, pt_ref, hi_ref, lo_ref, out_own_ref, grad_own_ref, out_partner_ref, grad_partner_ref,
    out_rows_ref, grad_rows_ref, mixed_ref, plain_ref,
):
    step = pl.program_id(0)
    size, width = BLOCK * CHUNKS, large_ref.shape[1]
    early = out_rows_ref.shape[0] * EARLY // PER_CHIP

    @pl.when(step == 0)
    def _():
        mixed_ref[...] = permutation(False, True)
        plain_ref[...] = permutation(False, False)

    pairs = large_ref.shape[0] // (2 * size)
    for i in range(pairs):
        mixed_from_wire(large_ref, i * 2 * size, mixed_ref[...], step * pairs + i, early, grad_rows_ref, out_rows_ref)
    for i in range(small_ref.shape[0] // size):
        start = early + step * (small_ref.shape[0] // CHUNKS) + i * BLOCK
        plain_from_wire(small_ref, i * size, plain_ref[...], out_rows_ref, start)

    @pl.when(step == pl.num_programs(0) - 1)
    def _():
        count = out_own_ref.shape[0]
        for c in range(CHUNKS):
            at = slice(c * width, (c + 1) * width)
            rows = out_rows_ref[:, at]
            total = dot(hi_ref[...], rows) + dot(lo_ref[...], rows)
            out_own_ref[:, at] = total[:count]
            out_partner_ref[:, at] = total[count:].astype(bf16)
            total = dot(pt_ref[...], grad_rows_ref[:, at])
            grad_own_ref[:, at] = total[:count]
            grad_partner_ref[:, at] = total[count:].astype(bf16)


def combine(small, large, matrices, slots, rows, features):
    size, width = BLOCK * CHUNKS, features // CHUNKS
    steps = small.shape[0] // (GROUP * LATE * CHUNKS)
    matrix_spec = pl.BlockSpec((2 * rows, slots), lambda i: (0, 0))
    part_spec = pl.BlockSpec((rows, features), lambda i: (0, 0))
    return pl.pallas_call(
        combine_kernel,
        grid=(steps,),
        in_specs=[
            pl.BlockSpec((GROUP * LATE * CHUNKS, width), lambda i: (i, 0)),
            pl.BlockSpec((GROUP * UNITS * CHUNKS, width), lambda i: (i, 0)),
        ]
        + [matrix_spec] * 3,
        out_specs=[part_spec] * 4,
        out_shape=[
            jax.ShapeDtypeStruct((rows, features), f32),
            jax.ShapeDtypeStruct((rows, features), f32),
            jax.ShapeDtypeStruct((rows, features), bf16),
            jax.ShapeDtypeStruct((rows, features), bf16),
        ],
        scratch_shapes=[
            pltpu.VMEM((slots, features), bf16),
            pltpu.VMEM((slots, features), bf16),
            pltpu.VMEM((size, size), bf16),
            pltpu.VMEM((size, size), bf16),
        ],
        compiler_params=pltpu.CompilerParams(vmem_limit_bytes=SMALL_LIMIT),
        cost_estimate=pl.CostEstimate(
            flops=4 * slots * (3 * rows + size) * features,
            bytes_accessed=4 * slots * features + 16 * rows * features,
            transcendentals=0,
        ),
    )(small, large, *matrices)


def local(tokens, grad_out, routes, gates, gate_weight, up_weight, down_weight):
    rows, features = tokens.shape
    units = gate_weight.shape[2]
    chips = lax.axis_size("dev")
    slots = chips * PER_CHIP
    role = lax.axis_index("role").astype(jnp.int32).reshape(1)
    swap = [(0, 1), (1, 0)]

    def other(array):
        return lax.ppermute(array, "role", swap)

    def exchange(wire):
        parts = wire.reshape(chips, wire.shape[0] // chips, wire.shape[1])
        parts = lax.all_to_all(parts, "dev", split_axis=0, concat_axis=0, tiled=True)
        return parts.reshape(wire.shape)

    route_lanes, gate_lanes = routes.T, gates.T
    route_other, gate_other = other(route_lanes), other(gate_lanes)
    p, slot_gate, *matrices = route(role, (route_lanes, route_other), (gate_lanes, gate_other), chips, slots)
    late_grad, _, _ = lax.optimization_barrier((grad_out, route_other, gate_other))
    large, small = pack(p, slot_gate, (tokens, other(tokens)), (grad_out, other(late_grad)), chips, slots)
    gate_local, up_local, down_local = gate_weight[0], up_weight[0], down_weight[0]

    large_in = exchange(large)
    small, _ = lax.optimization_barrier((small, large_in))
    small_in = exchange(small)
    small_out, out_early, grad_early, hidden_a, hidden_b = expert_call(
        True, (large_in, gate_local, up_local, down_local), slots, features, units
    )
    small_back = exchange(small_out)
    large_out = expert_call(
        False,
        (small_in, grad_early, out_early, hidden_a, hidden_b, down_local, gate_local, up_local),
        slots, features, units,
    )
    large_out, _ = lax.optimization_barrier((large_out, small_back))
    large_back = exchange(large_out)

    out_own, grad_own, out_partner, grad_partner = combine(small_back, large_back, matrices, slots, rows, features)
    out_received, grad_received = other(out_partner).astype(f32), other(grad_partner).astype(f32)
    tokens_wide = tokens.astype(f32)
    layer_out = (tokens_wide + (out_own + out_received)).astype(bf16)
    grad_normed = grad_own + grad_received
    inv_rms = lax.rsqrt(jnp.mean(tokens_wide * tokens_wide, axis=1, keepdims=True) + epsilon)
    projected = jnp.mean(grad_normed * tokens_wide, axis=1, keepdims=True)
    grad_in = grad_out.astype(f32) + inv_rms * grad_normed - tokens_wide * inv_rms**3 * projected
    return (layer_out, grad_in.astype(bf16))


def solution(mesh):
    split = P(("role", "dev"), None)
    split_weight = P(("role", "dev"), None, None)
    in_specs = (split, split, split, split, split_weight, split_weight, split_weight)
    return jax.shard_map(local, mesh=mesh, in_specs=in_specs, out_specs=(split, split), check_vma=False)
```
